32 devices in a mesh: hid: 8 (over z, x), mod: 4 (over y, core).
Axes of the slice: x: 2, y: 2, z: 4, core: 2. Of those that a mesh axis runs over, the one named last changes fastest.
Arguments:
- tokens: bfloat16 [128, 8192], P('hid', 'mod'), may hold values from -6 to 6
- grad_output: bfloat16 [128, 8192], P('hid', 'mod'), may hold values from -6 to 6
- gate_weight: bfloat16 [8192, 28672], P('mod', 'hid'), may hold values from -0.0625 to 0.0625
- up_weight: bfloat16 [8192, 28672], P('mod', 'hid'), may hold values from -0.0625 to 0.0625
- down_weight: bfloat16 [28672, 8192], P('hid', 'mod'), may hold values from -0.03125 to 0.03125
Outputs:
- grad_tokens: bfloat16 [128, 8192], P('hid', 'mod')
- grad_gate: bfloat16 [8192, 28672], P('mod', 'hid')
- grad_up: bfloat16 [8192, 28672], P('mod', 'hid')
- grad_down: bfloat16 [28672, 8192], P('hid', 'mod')
The draws below stay inside these ranges and needn't reach their ends.
All inputs are finite; a program needn't handle non-finite values.
Results may differ from the reference program's by a relative error of at most 0.0049.
Values may be sent and summed in bfloat16 or wider, within the bound.
No kernel may reach another device: no remote copies, remote signals or barrier semaphores. Data moves between devices by JAX's collectives and lax.ppermute only.
A program may use at most 128 MiB of HBM per device.

```python
import jax
import jax.numpy as jnp
from jax import lax

D = 8192
FF = 28672
TOKENS = 128


def shard_levels(stream_key, extent, cuts, smallest, largest):
    def one(dim, parts):
        steps = jax.random.uniform(jax.random.fold_in(jax.random.fold_in(stream_key, 6), dim), (parts,), jnp.float32, smallest / len(cuts), largest / len(cuts))
        return jnp.repeat(jnp.exp(steps), extent[dim] // parts).reshape((-1,) + (1,) * (len(extent) - dim - 1))

    loudness = one(*cuts[0])
    for cut in cuts[1:]:
        loudness = loudness * one(*cut)
    return loudness


def scatter_about(own_key, dims, spread, limit, cuts=(), dtype=jnp.bfloat16):
    gain = shard_levels(own_key, dims, cuts, -0.22, 0.18) if cuts else 1.0
    result = jax.random.normal(own_key, dims, jnp.float32) * spread * gain
    return jnp.minimum(jnp.maximum(result, -limit), limit).astype(dtype)


def setup_inputs(seed: int = 0) -> dict:
    arg_keys = jax.random.split(jax.random.key(seed), 6)
    tokens = scatter_about(arg_keys[0], (TOKENS, D), 1.0, 6.0, ((0, 8), (1, 4)))
    grad_output = scatter_about(arg_keys[1], (TOKENS, D), 1.0, 6.0, ((0, 8), (1, 4)))
    gate_weight = scatter_about(arg_keys[2], (D, FF), D ** -0.5, 0.0625, ((0, 4), (1, 8)))
    up_weight = scatter_about(arg_keys[3], (D, FF), D ** -0.5, 0.0625, ((0, 4), (1, 8)))
    down_weight = scatter_about(arg_keys[4], (FF, D), FF ** -0.5, 0.03125, ((0, 8), (1, 4)))
    return dict(tokens=tokens, grad_output=grad_output, gate_weight=gate_weight, up_weight=up_weight, down_weight=down_weight)


def swiglu_back(gate, up, grad_hidden):
    sigmoid_gate = jax.nn.sigmoid(gate)
    active = gate * sigmoid_gate
    hidden = (active * up).astype(jnp.bfloat16)
    up_back = (grad_hidden * active).astype(jnp.bfloat16)
    slope = sigmoid_gate * (1.0 + gate * (1.0 - sigmoid_gate))
    gate_back = (grad_hidden * up * slope).astype(jnp.bfloat16)
    return hidden, gate_back, up_back


def reference(tokens, grad_output, gate_weight, up_weight, down_weight):
    gate = jnp.dot(tokens, gate_weight, preferred_element_type=jnp.float32)
    up = jnp.dot(tokens, up_weight, preferred_element_type=jnp.float32)
    grad_hidden = lax.dot_general(grad_output, down_weight, (((1,), (1,)), ((), ())), preferred_element_type=jnp.float32)
    hidden, gate_back, up_back = swiglu_back(gate, up, grad_hidden)
    contract_rows = (((0,), (0,)), ((), ()))
    grad_down = lax.dot_general(hidden, grad_output, contract_rows, preferred_element_type=jnp.float32).astype(jnp.bfloat16)
    grad_gate = lax.dot_general(tokens, gate_back, contract_rows, preferred_element_type=jnp.float32).astype(jnp.bfloat16)
    grad_up = lax.dot_general(tokens, up_back, contract_rows, preferred_element_type=jnp.float32).astype(jnp.bfloat16)
    contract_cols = (((1,), (1,)), ((), ()))
    total = lax.dot_general(gate_back, gate_weight, contract_cols, preferred_element_type=jnp.float32)
    total = total + lax.dot_general(up_back, up_weight, contract_cols, preferred_element_type=jnp.float32)
    grad_tokens = total.astype(jnp.bfloat16)
    return grad_tokens, grad_gate, grad_up, grad_down
```

```python
import functools

import jax
import jax.numpy as jnp
from jax import lax
from jax.experimental import pallas as pl
from jax.experimental.pallas import tpu as pltpu
from jax.sharding import PartitionSpec as P

F32 = jnp.float32
BF16 = jnp.bfloat16
ROWS = (((1,), (0,)), ((), ()))
COLS = (((1,), (1,)), ((), ()))
GATE_EDGES = (0, 6, 8, 11, 13, 14)
DOWN_EDGES = (0, 0, 6, 8, 11, 14)
SPAN_EDGES = (0, 6, 11, 14)
ANYWHERE = pl.BlockSpec(memory_space=pl.ANY)
RESIDENT = pl.BlockSpec(memory_space=pltpu.VMEM)


def params(mib):
    return pltpu.CompilerParams(vmem_limit_bytes=mib * 2**20)


def cost(macs, nbytes, scale=1):
    return pl.CostEstimate(
        flops=2 * macs // scale, bytes_accessed=nbytes // scale, transcendentals=0
    )


def pinned(weight):
    return pltpu.with_memory_space_constraint(weight, pltpu.HBM)


def forward_kernel(jobs, tile, kinds, *refs):
    n = len(kinds)
    rows = dict(zip(sorted({kind for kind, _ in kinds}), refs))
    weights = dict(zip(kinds, refs[len(rows) : len(rows) + n]))
    keep, send, tall, wide, sems = refs[-5:]
    half = keep.shape[0]
    steps, used = [], [0, 0]
    for (kind, name), first, tiles in jobs:
        for i in range(tiles):
            take = pl.ds((first + i) * tile, tile)
            down = int(kind == "g")
            source = weights[(kind, name)].at[(take,) if down else (slice(None), take)]
            target = (tall, wide)[down].at[used[down]]
            used[down] += 1
            steps.append((kind, target, pltpu.make_async_copy(source, target, sems.at[len(steps)])))
    for _, _, copy in steps:
        copy.start()
    for i, (kind, target, copy) in enumerate(steps):
        copy.wait()
        value = lax.dot_general(
            rows[kind][...],
            target[...],
            ROWS if kind == "x" else COLS,
            preferred_element_type=F32,
        )
        put = pl.ds(i * tile, tile)
        keep[:, put] = value[:half]
        send[:, put] = value[half:].astype(BF16)


def forward_part(rows, weights, jobs, tile, after=()):
    kinds = sorted({key for key, _, _ in jobs})
    used = [rows[kind] for kind in sorted({kind for kind, _ in kinds})]
    t, d = used[0].shape
    n_wide = sum(tiles for key, _, tiles in jobs if key[0] == "g")
    n_tall = sum(tiles for key, _, tiles in jobs if key[0] == "x")
    total = (n_wide + n_tall) * tile
    return pl.pallas_call(
        functools.partial(forward_kernel, jobs, tile, kinds),
        in_specs=[RESIDENT] * len(used) + [ANYWHERE] * (len(kinds) + len(after)),
        out_specs=[RESIDENT] * 2,
        out_shape=[
            jax.ShapeDtypeStruct((t // 2, total), F32),
            jax.ShapeDtypeStruct((t // 2, total), BF16),
        ],
        scratch_shapes=[
            pltpu.VMEM((max(n_tall, 1), d, tile), BF16),
            pltpu.VMEM((max(n_wide, 1), tile, d), BF16),
            pltpu.SemaphoreType.DMA((n_tall + n_wide,)),
        ],
        compiler_params=params(28),
        cost_estimate=cost(2 * t * d * total, 2 * d * total, 32),
        name="forward_part",
    )(*used, *[weights[key] for key in kinds], *after)


def step_of(d):
    return 512 if d % 512 == 0 else d


def joined(mine, peer, slot):
    return jnp.concatenate([mine[slot], peer[slot]], axis=0)


def input_kernel(has_prev, first, *refs):
    mine, peer, wg, wu, *others = refs
    prev = others[0]
    out, gate_buf, up_buf, sems = refs[-4:]
    step = step_of(out.shape[1])
    parts = [pl.ds(at, step) for at in range(0, out.shape[1], step)]
    cols = pl.ds(first, mine.shape[2])
    copies = [
        (
            pltpu.make_async_copy(wg.at[part, cols], gate_buf.at[part], sems.at[0, i]),
            pltpu.make_async_copy(wu.at[part, cols], up_buf.at[part], sems.at[1, i]),
        )
        for i, part in enumerate(parts)
    ]
    for pair in copies:
        for copy in pair:
            copy.start()
    gb = joined(mine, peer, 1)
    ub = joined(mine, peer, 2)
    for part, pair in zip(parts, copies):
        pair[0].wait()
        value = lax.dot_general(gb, gate_buf[part, :], COLS, preferred_element_type=F32)
        pair[1].wait()
        value += lax.dot_general(ub, up_buf[part, :], COLS, preferred_element_type=F32)
        out[:, part] = value + prev[:, part] if has_prev else value


def input_part(prev, mine, peer, wg, wu, first, after):
    t, d, span = 2 * mine.shape[1], wg.shape[0], mine.shape[2]
    has_prev = prev is not None
    return pl.pallas_call(
        functools.partial(input_kernel, has_prev, first),
        in_specs=[RESIDENT] * 2
        + [ANYWHERE] * 2
        + [RESIDENT] * int(has_prev)
        + [ANYWHERE] * len(after),
        out_specs=RESIDENT,
        out_shape=jax.ShapeDtypeStruct((t, d), F32),
        scratch_shapes=[
            pltpu.VMEM((d, span), BF16),
            pltpu.VMEM((d, span), BF16),
            pltpu.SemaphoreType.DMA((2, d // step_of(d))),
        ],
        compiler_params=params(28),
        cost_estimate=cost(2 * t * d * span, 4 * d * span),
        name="input_part",
    )(mine, peer, wg, wu, *([prev] if has_prev else []), *after)


def weight_kernel(firsts, tile, *refs):
    n = len(firsts)
    x, g = refs[:2]
    acts = [(refs[2 + 2 * i], refs[3 + 2 * i]) for i in range(n)]
    grad_gate, grad_up, grad_down, xt, gate_buf, up_buf, down_buf, sems = refs[-8:]
    d = x.shape[1]
    step = step_of(d)
    xt[...] = x[...].T
    copies = []

    def out(source, target):
        copy = pltpu.make_async_copy(source, target, sems.at[len(copies)])
        copy.start()
        copies.append(copy)

    start = 0
    for first, (mine, peer) in zip(firsts, acts):
        span = mine.shape[2]
        held, cols = pl.ds(start, span), pl.ds(first, span)
        gb = joined(mine, peer, 1)
        ub = joined(mine, peer, 2)
        ht = joined(mine, peer, 0).T
        for at in range(0, d, step):
            part = pl.ds(at, step)
            rows = xt[part, :]
            for value, buf, grad in ((gb, gate_buf, grad_gate), (ub, up_buf, grad_up)):
                buf[part, held] = lax.dot_general(
                    rows, value, ROWS, preferred_element_type=F32
                ).astype(BF16)
                out(buf.at[part, held], grad.at[part, cols])
        for at in range(0, span, tile):
            part = pl.ds(start + at, tile)
            down_buf[part, :] = lax.dot_general(
                ht[at : at + tile], g[...], ROWS, preferred_element_type=F32
            ).astype(BF16)
            out(down_buf.at[part], grad_down.at[pl.ds(first + at, tile)])
        start += span
    for copy in copies:
        copy.wait()


def weight_part(prev, x, g, acts, firsts, tile, hidden, after):
    t, d = x.shape
    prev = [] if prev is None else list(prev)
    spans = [mine.shape[2] for mine, _ in acts]
    total = sum(spans)
    n_copies = len(acts) * 2 * (d // step_of(d)) + total // tile
    flat = [array for pair in acts for array in pair]
    return pl.pallas_call(
        functools.partial(weight_kernel, firsts, tile),
        in_specs=[RESIDENT] * (2 + len(flat)) + [ANYWHERE] * (len(prev) + len(after)),
        out_specs=[ANYWHERE] * 3,
        out_shape=[
            jax.ShapeDtypeStruct((d, hidden), BF16),
            jax.ShapeDtypeStruct((d, hidden), BF16),
            jax.ShapeDtypeStruct((hidden, d), BF16),
        ],
        scratch_shapes=[
            pltpu.VMEM((d, t), BF16),
            pltpu.VMEM((d, total), BF16),
            pltpu.VMEM((d, total), BF16),
            pltpu.VMEM((total, d), BF16),
            pltpu.SemaphoreType.DMA((n_copies,)),
        ],
        input_output_aliases={2 + len(flat) + i: i for i in range(len(prev))},
        compiler_params=params(34),
        cost_estimate=cost(3 * t * d * total, 6 * d * total),
        name="weight_part",
    )(x, g, *flat, *prev, *after)


def add_kernel(keep, got, *refs):
    refs[-1][...] = (keep[...] + got[...].astype(F32)).astype(BF16)


def add_part(keep, got, after=()):
    return pl.pallas_call(
        add_kernel,
        in_specs=[RESIDENT] * 2 + [ANYWHERE] * len(after),
        out_specs=RESIDENT,
        out_shape=jax.ShapeDtypeStruct(keep.shape, BF16),
        compiler_params=params(16),
        cost_estimate=cost(keep.size, 8 * keep.size),
        name="add_part",
    )(keep, got, *after)


def swiglu_kernel(places, tile, n_sums, *refs):
    out = refs[-1]
    for i, place in enumerate(places):
        gate, up, grad_hidden = (
            refs[which * n_sums][:, pl.ds(first, tile)]
            + sum(
                refs[which * n_sums + j][:, pl.ds(first, tile)].astype(F32)
                for j in range(1, n_sums)
            )
            for which, first in place
        )
        sigmoid_gate = jax.nn.sigmoid(gate)
        active = gate * sigmoid_gate
        slope = sigmoid_gate * (1.0 + gate * (1.0 - sigmoid_gate))
        part = pl.ds(i * tile, tile)
        out[0, :, part] = (active * up).astype(BF16)
        out[1, :, part] = (grad_hidden * up * slope).astype(BF16)
        out[2, :, part] = (grad_hidden * active).astype(BF16)


def swiglu_part(places, pieces, tile, after=()):
    width = len(places) * tile
    flat = [array for piece in pieces for array in piece]
    rows = flat[0].shape[0]
    return pl.pallas_call(
        functools.partial(swiglu_kernel, places, tile, len(pieces[0])),
        in_specs=[RESIDENT] * len(flat) + [ANYWHERE] * len(after),
        out_specs=RESIDENT,
        out_shape=jax.ShapeDtypeStruct((3, rows, width), BF16),
        compiler_params=params(20),
        cost_estimate=cost(20 * rows * width, 14 * rows * width),
        name="swiglu_part",
    )(*flat, *after)


def shards(n_hid, n_mod, tokens, grad_output, gate_weight, up_weight, down_weight):
    hidden = gate_weight.shape[1]
    rows = tokens.shape[0]
    far = n_hid // 2
    core = lax.axis_index("mod") % 2

    def swap(value, axis, size, bit):
        return lax.ppermute(value, axis, [(i ^ bit, i) for i in range(size)])

    def from_far(value, k):
        return swap(value, "hid", n_hid, 2 * k)

    def near(value):
        return swap(value, "hid", n_hid, 1)

    def other_core(value):
        return swap(value, "mod", n_mod, 1)

    def along(block):
        return [block] + [from_far(block, k) for k in range(1, far)]

    def across(column):
        own = jnp.concatenate(column, axis=0)
        theirs = near(own)
        return jnp.concatenate(
            [jnp.where(core == 0, own, theirs), jnp.where(core == 0, theirs, own)], axis=0
        )

    column = along(tokens)
    held, _ = lax.optimization_barrier((grad_output, column))
    x = across(column)
    g = across(along(held))
    gate_key, up_key, down_key = ("x", 0), ("x", 1), ("g", 2)
    weights = {
        gate_key: pinned(gate_weight),
        up_key: pinned(up_weight),
        down_key: pinned(down_weight),
    }

    tile = next((n for n in (256, 128) if hidden % n == 0), hidden)
    n_tiles = hidden // tile

    def ranges(edges):
        bounds = [round(e * n_tiles / edges[-1]) for e in edges]
        return list(zip(bounds[:-1], bounds[1:]))

    spans = [(a, b) for a, b in ranges(SPAN_EDGES) if b > a]

    def exchanged(jobs, after=()):
        keep, send = forward_part({"x": x, "g": g}, weights, jobs, tile, after)
        got = other_core(send)
        narrow = add_part(keep, got)
        others = [swap(narrow, "mod", n_mod, 2 * k) for k in range(1, n_mod // 2)]
        return (keep, got, *others), send, narrow

    n = len(spans)
    pieces, sends, narrows = [], [], []
    where = {gate_key: [], up_key: [], down_key: []}
    for (a, b), (c, d) in zip(ranges(GATE_EDGES), ranges(DOWN_EDGES)):
        jobs = [(gate_key, a, b - a), (up_key, a, b - a), (down_key, c, d - c)]
        jobs = [job for job in jobs if job[2]]
        if not jobs:
            continue
        k, at = len(pieces), 0
        for key, _, tiles in jobs:
            where[key] += [(k, at + i * tile) for i in range(tiles)]
            at += tiles * tile
        after = narrows[-1:] + [piece[-1] for piece in pieces[-2:-1]]
        for held, value in zip((pieces, sends, narrows), exchanged(jobs, after)):
            held.append(value)

    def act(i, after=()):
        places = list(zip(*(where[key][slice(*spans[i])] for key in (gate_key, up_key, down_key))))
        used = sorted({which for place in places for which, _ in place})
        local = [[(used.index(which), first) for which, first in place] for place in places]
        mine = swiglu_part(local, [pieces[which] for which in used], tile, after)
        return mine, other_core(mine)

    def weight_grads(prev, group, after):
        return weight_part(
            prev,
            x,
            g,
            [acts[j] for j in group],
            [spans[j][0] * tile for j in group],
            tile,
            hidden,
            after,
        )

    def tokens_grad(prev, i, after):
        mine, peer = acts[i]
        first = spans[i][0] * tile
        return input_part(prev, mine, peer, weights[gate_key], weights[up_key], first, after)

    acts = [act(0, sends[-1:])]
    waited = [piece[-1] for piece in pieces[-2:-1]]
    total = tokens_grad(None, 0, narrows[-1:] + waited)
    for i in range(1, n):
        acts.append(act(i, [total] if i == 1 else [acts[-1][0]]))
    for i in range(1, n):
        total = tokens_grad(total, i, [acts[-1][0]])

    half = total.shape[0] // 2
    top, bottom = total[:half], total[half:]
    own = jnp.where(core == 0, top, bottom)
    theirs = jnp.where(core == 0, bottom, top).astype(BF16)
    own = own + near(theirs).astype(F32)
    result = own[:rows]
    for k in range(1, far):
        block = own[k * rows : (k + 1) * rows].astype(BF16)
        result = result + from_far(block, k).astype(F32)

    grads = None
    for group in ([0], list(range(1, n))):
        if group:
            grads = weight_grads(grads, group, [theirs])
    grad_gate, grad_up, grad_down = grads
    return (result.astype(BF16), grad_gate, grad_up, grad_down)


def solution(mesh):
    placed = (P("hid", "mod"), P("hid", "mod"), P("mod", "hid"), P("mod", "hid"), P("hid", "mod"))
    return jax.shard_map(
        functools.partial(shards, mesh.shape["hid"], mesh.shape["mod"]),
        mesh=mesh,
        in_specs=placed,
        out_specs=(P("hid", "mod"), P("mod", "hid"), P("mod", "hid"), P("hid", "mod")),
        check_vma=False,
    )
```

```python
import functools

import jax
import jax.numpy as jnp
from jax import lax
from jax.experimental import pallas as pl
from jax.experimental.pallas import tpu as pltpu
from jax.sharding import PartitionSpec as P

F32 = jnp.float32
BF16 = jnp.bfloat16
ROWS = (((1,), (0,)), ((), ()))
COLS = (((1,), (1,)), ((), ()))
GATE_EDGES = (0, 7, 9, 12, 14)
DOWN_EDGES = (0, 0, 7, 10, 14)
SPAN_EDGES = (0, 7, 14)
FLIGHT = 6
ANYWHERE = pl.BlockSpec(memory_space=pl.ANY)
RESIDENT = pl.BlockSpec(memory_space=pltpu.VMEM)


def params(mib):
    return pltpu.CompilerParams(vmem_limit_bytes=mib * 2**20)


def cost(macs, nbytes, scale=1):
    return pl.CostEstimate(
        flops=2 * macs // scale, bytes_accessed=nbytes // scale, transcendentals=0
    )


def pinned(weight):
    return pltpu.with_memory_space_constraint(weight, pltpu.HBM)


def row_blocks(d):
    step = step_of(d)
    return [pl.ds(at, step) for at in range(0, d, step)]


def load_kernel(first, gate, up, gate_out, up_out, mark, sems):
    mark[...] = jnp.zeros_like(mark)
    take = pl.ds(first, gate_out.shape[1])
    copies = [
        pltpu.make_async_copy(source.at[part, take], target.at[part], sems.at[which, i])
        for which, (source, target) in enumerate(((gate, gate_out), (up, up_out)))
        for i, part in enumerate(row_blocks(gate.shape[0]))
    ]
    for copy in copies:
        copy.start()
    for copy in copies:
        copy.wait()


def load_part(gate, up, first, width):
    d = gate.shape[0]
    loaded = pl.pallas_call(
        functools.partial(load_kernel, first),
        in_specs=[ANYWHERE] * 2,
        out_specs=[RESIDENT] * 3,
        out_shape=[pltpu.VMEM((d, width), BF16)] * 2 + [jax.ShapeDtypeStruct((8, 128), F32)],
        scratch_shapes=[pltpu.SemaphoreType.DMA((2, len(row_blocks(d))))],
        compiler_params=params(2),
        cost_estimate=cost(0, 4 * d * width),
        name="load_part",
    )(gate, up)
    *values, mark = loaded
    return [pltpu.with_memory_space_constraint(value, pltpu.VMEM) for value in values], mark


def stack_kernel(n, *refs):
    out = refs[-1]
    rows = refs[0].shape[0]
    for i in range(n):
        out[pl.ds(i * rows, rows), :] = refs[i][...]


def stack_part(blocks, after):
    rows, d = blocks[0].shape
    return pl.pallas_call(
        functools.partial(stack_kernel, len(blocks)),
        in_specs=[RESIDENT] * len(blocks) + [ANYWHERE] * len(after),
        out_specs=RESIDENT,
        out_shape=jax.ShapeDtypeStruct((len(blocks) * rows, d), BF16),
        compiler_params=params(12),
        cost_estimate=cost(0, 4 * rows * d, 32),
        name="stack_part",
    )(*blocks, *after)


def join_kernel(own, theirs, out, turned):
    half = own.shape[0]
    core = lax.rem(lax.axis_index("mod"), 2)
    out[pl.ds(pl.multiple_of(core * half, half), half), :] = own[...]
    out[pl.ds(pl.multiple_of((1 - core) * half, half), half), :] = theirs[...]
    turned[...] = out[...].T


def join_part(own, theirs):
    half, d = own.shape
    return pl.pallas_call(
        join_kernel,
        in_specs=[RESIDENT] * 2,
        out_specs=[RESIDENT] * 2,
        out_shape=[
            jax.ShapeDtypeStruct((2 * half, d), BF16),
            jax.ShapeDtypeStruct((d, 2 * half), BF16),
        ],
        compiler_params=params(24),
        cost_estimate=cost(0, 8 * half * d, 32),
        name="join_part",
    )(own, theirs)


def split_rows(value, keep, send, at):
    half = keep.shape[0]
    put = pl.ds(at, value.shape[1])
    keep[:, put] = value[:half]
    send[:, put] = value[half:].astype(BF16)


def first_kernel(tile, has_prev, x, weight, *refs):
    keep, send = refs[-2:]
    width = weight.shape[1]
    if has_prev:
        keep[:, :width] = refs[0][:, :width]
        send[:, :width] = refs[1][:, :width]
    start = width if has_prev else 0
    for at in range(0, width, tile):
        value = lax.dot_general(
            x[...], weight[:, pl.ds(at, tile)], ROWS, preferred_element_type=F32
        )
        split_rows(value, keep, send, start + at)


def piece_shapes(tokens, total):
    return [
        jax.ShapeDtypeStruct((tokens // 2, total), F32),
        jax.ShapeDtypeStruct((tokens // 2, total), BF16),
    ]


def first_part(x, weight, prev, tile, after):
    t, d = x.shape
    width = weight.shape[1]
    return pl.pallas_call(
        functools.partial(first_kernel, tile, len(prev) > 0),
        in_specs=[RESIDENT] * (2 + len(prev)) + [ANYWHERE] * len(after),
        out_specs=[RESIDENT] * 2,
        out_shape=piece_shapes(t, 2 * width),
        compiler_params=params(8),
        cost_estimate=cost(t * d * width, 2 * d * width, 32),
        name="first_part",
    )(x, weight, *prev, *after)


def forward_kernel(jobs, tile, kinds, *refs):
    n = len(kinds)
    rows = dict(zip(sorted({kind for kind, _ in kinds}), refs))
    weights = dict(zip(kinds, refs[len(rows) : len(rows) + n]))
    keep, send, tall, wide, sums, sems = refs[-6:]
    blocks = row_blocks(tall.shape[0])
    steps, start, used = [], 0, 0

    def step(source, target, work):
        steps.append((pltpu.make_async_copy(source, target, sems.at[len(steps)]), work))

    def tall_work(i, part, at, width):
        for col in range(at, at + width, tile):
            put = pl.ds(col, tile)
            value = lax.dot_general(
                rows["x"][:, part], tall[part, put], ROWS, preferred_element_type=F32
            )
            if i:
                value += sums[:, put]
            if i + 1 < len(blocks):
                sums[:, put] = value
            else:
                split_rows(value, keep, send, col)

    def wide_work(target, at):
        value = lax.dot_general(target[...], rows["g"][...], ROWS, preferred_element_type=F32)
        split_rows(value.T, keep, send, at)

    for (kind, name), first, tiles in jobs:
        weight, width = weights[(kind, name)], tiles * tile
        if kind == "x":
            put = pl.ds(start, width)
            for i, part in enumerate(blocks):
                source = weight.at[part, pl.ds(first * tile, width)]
                work = functools.partial(tall_work, i, part, start, width)
                step(source, tall.at[part, put], work)
        else:
            for i in range(tiles):
                source = weight.at[pl.ds((first + i) * tile, tile)]
                target = wide.at[used]
                step(source, target, functools.partial(wide_work, target, start + i * tile))
                used += 1
        start += width
    for copy, _ in steps[:FLIGHT]:
        copy.start()
    for i, (copy, work) in enumerate(steps):
        copy.wait()
        for later, _ in steps[i + FLIGHT : i + FLIGHT + 1]:
            later.start()
        work()


def forward_part(rows, weights, jobs, tile, half, after=()):
    kinds = sorted({key for key, _, _ in jobs})
    used = [rows[kind] for kind in sorted({kind for kind, _ in kinds})]
    d, t = weights[kinds[0]].shape[1 if kinds[0][0] == "g" else 0], 2 * half
    n_wide = sum(tiles for key, _, tiles in jobs if key[0] == "g")
    tall_jobs = [tiles for key, _, tiles in jobs if key[0] == "x"]
    tall_width = max(sum(tall_jobs), 1) * tile
    total = (n_wide + sum(tall_jobs)) * tile
    return pl.pallas_call(
        functools.partial(forward_kernel, jobs, tile, kinds),
        in_specs=[RESIDENT] * len(used) + [ANYWHERE] * (len(kinds) + len(after)),
        out_specs=[RESIDENT] * 2,
        out_shape=piece_shapes(t, total),
        scratch_shapes=[
            pltpu.VMEM((d, tall_width), BF16),
            pltpu.VMEM((max(n_wide, 1), tile, d), BF16),
            pltpu.VMEM((t, tall_width), F32),
            pltpu.SemaphoreType.DMA((n_wide + len(tall_jobs) * len(row_blocks(d)),)),
        ],
        compiler_params=params(28),
        cost_estimate=cost(2 * t * d * total, 2 * d * total, 32),
        name="forward_part",
    )(*used, *[weights[key] for key in kinds], *after)


def step_of(d):
    return 512 if d % 512 == 0 else d


def joined(mine, peer, slot):
    return jnp.concatenate([mine[slot], peer[slot]], axis=0)


def input_kernel(has_prev, first, *refs):
    mine, peer, wg, wu, *others = refs
    prev = others[0]
    out, gate_buf, up_buf, sems = refs[-4:]
    parts = row_blocks(wg.shape[0])
    cols = pl.ds(first, mine.shape[2])
    copies = [
        (
            pltpu.make_async_copy(wg.at[part, cols], gate_buf.at[part], sems.at[0, i]),
            pltpu.make_async_copy(wu.at[part, cols], up_buf.at[part], sems.at[1, i]),
        )
        for i, part in enumerate(parts)
    ]
    for pair in copies[: FLIGHT // 2]:
        for copy in pair:
            copy.start()
    gb = joined(mine, peer, 1)
    ub = joined(mine, peer, 2)
    for i, (part, pair) in enumerate(zip(parts, copies)):
        for copy in pair:
            copy.wait()
        for later in copies[i + FLIGHT // 2 : i + FLIGHT // 2 + 1]:
            for copy in later:
                copy.start()
        value = lax.dot_general(gb, gate_buf[part, :], COLS, preferred_element_type=F32)
        value += lax.dot_general(ub, up_buf[part, :], COLS, preferred_element_type=F32)
        out[:, part] = value + prev[:, part] if has_prev else value


def input_part(prev, mine, peer, wg, wu, first, after):
    t, d, span = 2 * mine.shape[1], wg.shape[0], mine.shape[2]
    has_prev = prev is not None
    return pl.pallas_call(
        functools.partial(input_kernel, has_prev, first),
        in_specs=[RESIDENT] * 2
        + [ANYWHERE] * 2
        + [RESIDENT] * int(has_prev)
        + [ANYWHERE] * len(after),
        out_specs=RESIDENT,
        out_shape=jax.ShapeDtypeStruct((t, d), F32),
        scratch_shapes=[
            pltpu.VMEM((d, span), BF16),
            pltpu.VMEM((d, span), BF16),
            pltpu.SemaphoreType.DMA((2, len(row_blocks(d)))),
        ],
        compiler_params=params(28),
        cost_estimate=cost(2 * t * d * span, 4 * d * span),
        name="input_part",
    )(mine, peer, wg, wu, *([prev] if has_prev else []), *after)


def weight_kernel(firsts, tile, *refs):
    n = len(firsts)
    xt, g = refs[:2]
    acts = [(refs[2 + 2 * i], refs[3 + 2 * i]) for i in range(n)]
    grad_gate, grad_up, grad_down, gate_buf, up_buf, down_buf, sems = refs[-7:]
    d = xt.shape[0]
    step = step_of(d)
    copies = []

    def out(source, target):
        copy = pltpu.make_async_copy(source, target, sems.at[len(copies)])
        copy.start()
        copies.append(copy)

    start = 0
    for first, (mine, peer) in zip(firsts, acts):
        span = mine.shape[2]
        held, cols = pl.ds(start, span), pl.ds(first, span)
        gb = joined(mine, peer, 1)
        ub = joined(mine, peer, 2)
        ht = joined(mine, peer, 0).T
        for at in range(0, d, step):
            part = pl.ds(at, step)
            rows = xt[part, :]
            for value, buf, grad in ((gb, gate_buf, grad_gate), (ub, up_buf, grad_up)):
                buf[part, held] = lax.dot_general(
                    rows, value, ROWS, preferred_element_type=F32
                ).astype(BF16)
                out(buf.at[part, held], grad.at[part, cols])
        for at in range(0, span, tile):
            part = pl.ds(start + at, tile)
            down_buf[part, :] = lax.dot_general(
                ht[at : at + tile], g[...], ROWS, preferred_element_type=F32
            ).astype(BF16)
            out(down_buf.at[part], grad_down.at[pl.ds(first + at, tile)])
        start += span
    for copy in copies:
        copy.wait()


def weight_part(prev, xt, g, acts, firsts, tile, hidden, after):
    t, d = g.shape
    prev = [] if prev is None else list(prev)
    spans = [mine.shape[2] for mine, _ in acts]
    total = sum(spans)
    n_copies = len(acts) * 2 * (d // step_of(d)) + total // tile
    flat = [array for pair in acts for array in pair]
    return pl.pallas_call(
        functools.partial(weight_kernel, firsts, tile),
        in_specs=[RESIDENT] * (2 + len(flat)) + [ANYWHERE] * (len(prev) + len(after)),
        out_specs=[ANYWHERE] * 3,
        out_shape=[
            jax.ShapeDtypeStruct((d, hidden), BF16),
            jax.ShapeDtypeStruct((d, hidden), BF16),
            jax.ShapeDtypeStruct((hidden, d), BF16),
        ],
        scratch_shapes=[
            pltpu.VMEM((d, total), BF16),
            pltpu.VMEM((d, total), BF16),
            pltpu.VMEM((total, d), BF16),
            pltpu.SemaphoreType.DMA((n_copies,)),
        ],
        input_output_aliases={2 + len(flat) + i: i for i in range(len(prev))},
        compiler_params=params(34),
        cost_estimate=cost(3 * t * d * total, 6 * d * total),
        name="weight_part",
    )(xt, g, *flat, *prev, *after)


def add_kernel(keep, got, *refs):
    refs[-1][...] = (keep[...] + got[...].astype(F32)).astype(BF16)


def add_part(keep, got, after=()):
    return pl.pallas_call(
        add_kernel,
        in_specs=[RESIDENT] * 2 + [ANYWHERE] * len(after),
        out_specs=RESIDENT,
        out_shape=jax.ShapeDtypeStruct(keep.shape, BF16),
        compiler_params=params(16),
        cost_estimate=cost(keep.size, 8 * keep.size, 64),
        name="add_part",
    )(keep, got, *after)


def swiglu_kernel(places, tile, n_sums, *refs):
    out = refs[-1]
    for i, place in enumerate(places):
        gate, up, grad_hidden = (
            refs[which * n_sums][:, pl.ds(first, tile)]
            + sum(
                refs[which * n_sums + j][:, pl.ds(first, tile)].astype(F32)
                for j in range(1, n_sums)
            )
            for which, first in place
        )
        sigmoid_gate = jax.nn.sigmoid(gate)
        active = gate * sigmoid_gate
        slope = sigmoid_gate * (1.0 + gate * (1.0 - sigmoid_gate))
        part = pl.ds(i * tile, tile)
        out[0, :, part] = (active * up).astype(BF16)
        out[1, :, part] = (grad_hidden * up * slope).astype(BF16)
        out[2, :, part] = (grad_hidden * active).astype(BF16)


def swiglu_part(places, pieces, tile, after=()):
    width = len(places) * tile
    flat = [array for piece in pieces for array in piece]
    rows = flat[0].shape[0]
    return pl.pallas_call(
        functools.partial(swiglu_kernel, places, tile, len(pieces[0])),
        in_specs=[RESIDENT] * len(flat) + [ANYWHERE] * len(after),
        out_specs=RESIDENT,
        out_shape=jax.ShapeDtypeStruct((3, rows, width), BF16),
        compiler_params=params(20),
        cost_estimate=cost(20 * rows * width, 14 * rows * width, 64),
        name="swiglu_part",
    )(*flat, *after)


def shards(n_hid, n_mod, tokens, grad_output, gate_weight, up_weight, down_weight):
    hidden = gate_weight.shape[1]
    rows = tokens.shape[0]
    far = n_hid // 2
    core = lax.axis_index("mod") % 2

    def swap(value, axis, size, bit):
        return lax.ppermute(value, axis, [(i ^ bit, i) for i in range(size)])

    def from_far(value, k):
        return swap(value, "hid", n_hid, 2 * k)

    def near(value):
        return swap(value, "hid", n_hid, 1)

    def other_core(value):
        return swap(value, "mod", n_mod, 1)

    def along(block):
        return [block] + [from_far(block, k) for k in range(1, far)]

    def across(column, after):
        own = stack_part(column, after)
        return join_part(own, near(own))

    gate_key, up_key, down_key = ("x", 0), ("x", 1), ("g", 2)
    weights = {
        gate_key: pinned(gate_weight),
        up_key: pinned(up_weight),
        down_key: pinned(down_weight),
    }

    tile = next((n for n in (256, 128) if hidden % n == 0), hidden)
    n_tiles = hidden // tile

    def ranges(edges):
        bounds = [round(e * n_tiles / edges[-1]) for e in edges]
        return list(zip(bounds[:-1], bounds[1:]))

    spans = [(a, b) for a, b in ranges(SPAN_EDGES) if b > a]
    a, b = next((a, b) for a, b in ranges(GATE_EDGES) if b > a)
    loaded, mark = load_part(weights[gate_key], weights[up_key], a * tile, (b - a) * tile)

    x, x_turned = across(along(tokens), [mark])
    column = along(grad_output)
    rows_of = {"x": x}

    def exchanged(jobs, after=()):
        if pieces:
            keep, send = forward_part(rows_of, weights, jobs, tile, rows * far, after)
        else:
            half = first_part(x, loaded[0], [], tile, [])
            keep, send = first_part(x, loaded[1], half, tile, after)
        got = other_core(send)
        narrow = add_part(keep, got, pieces[-1][-1:] if len(pieces) == 3 else ())
        others = [swap(narrow, "mod", n_mod, 2 * k) for k in range(1, n_mod // 2)]
        return (keep, got, *others), send, narrow

    n = len(spans)
    pieces, sends, narrows = [], [], []
    where = {gate_key: [], up_key: [], down_key: []}
    for (a, b), (c, d) in zip(ranges(GATE_EDGES), ranges(DOWN_EDGES)):
        jobs = [(gate_key, a, b - a), (up_key, a, b - a), (down_key, c, d - c)]
        jobs = [job for job in jobs if job[2]]
        if not jobs:
            continue
        k, at = len(pieces), 0
        for key, _, tiles in jobs:
            where[key] += [(k, at + i * tile) for i in range(tiles)]
            at += tiles * tile
        after = narrows[-1:] + [piece[-1] for piece in pieces[-2:-1]]
        after = after if pieces else column[1:]
        for kept, value in zip((pieces, sends, narrows), exchanged(jobs, after)):
            kept.append(value)
        if k == 0:
            g, rows_of["g"] = across(column, sends[:1])

    def act(i, after=()):
        places = list(zip(*(where[key][slice(*spans[i])] for key in (gate_key, up_key, down_key))))
        used = sorted({which for place in places for which, _ in place})
        local = [[(used.index(which), first) for which, first in place] for place in places]
        mine = swiglu_part(local, [pieces[which] for which in used], tile, after)
        return mine, other_core(mine)

    def weight_grads(prev, group, after):
        return weight_part(
            prev,
            x_turned,
            g,
            [acts[j] for j in group],
            [spans[j][0] * tile for j in group],
            tile,
            hidden,
            after,
        )

    def tokens_grad(prev, i, after):
        mine, peer = acts[i]
        first = spans[i][0] * tile
        return input_part(prev, mine, peer, weights[gate_key], weights[up_key], first, after)

    acts = [act(0, narrows[-2:-1])]
    total = tokens_grad(None, 0, narrows[-1:])
    for i in range(1, n):
        acts.append(act(i, [total]))
    for i in range(1, n):
        total = tokens_grad(total, i, [])

    half = total.shape[0] // 2
    top, bottom = total[:half], total[half:]
    own = jnp.where(core == 0, top, bottom)
    theirs = jnp.where(core == 0, bottom, top).astype(BF16)
    own = own + near(theirs).astype(F32)
    result = own[:rows]
    for k in range(1, far):
        block = own[k * rows : (k + 1) * rows].astype(BF16)
        result = result + from_far(block, k).astype(F32)

    grads = None
    for group in ([0], list(range(1, n))):
        if group:
            grads = weight_grads(grads, group, [theirs])
    grad_gate, grad_up, grad_down = grads
    return (result.astype(BF16), grad_gate, grad_up, grad_down)


def solution(mesh):
    placed = (P("hid", "mod"), P("hid", "mod"), P("mod", "hid"), P("mod", "hid"), P("hid", "mod"))
    return jax.shard_map(
        functools.partial(shards, mesh.shape["hid"], mesh.shape["mod"]),
        mesh=mesh,
        in_specs=placed,
        out_specs=(P("hid", "mod"), P("mod", "hid"), P("mod", "hid"), P("hid", "mod")),
        check_vma=False,
    )
```

```python
import functools

import jax
import jax.numpy as jnp
from jax import lax
from jax.experimental import pallas as pl
from jax.experimental.pallas import tpu as pltpu
from jax.sharding import PartitionSpec as P

F32 = jnp.float32
BF16 = jnp.bfloat16
ROWS = (((1,), (0,)), ((), ()))
COLS = (((1,), (1,)), ((), ()))
GATE_EDGES = (0, 7, 13, 13, 14)
DOWN_EDGES = (0, 0, 0, 9, 14)
SPAN_EDGES = (0, 7, 14)
FLIGHT = 3
PAIRS = 2
ANYWHERE = pl.BlockSpec(memory_space=pl.ANY)
RESIDENT = pl.BlockSpec(memory_space=pltpu.VMEM)


def params(mib):
    return pltpu.CompilerParams(vmem_limit_bytes=mib * 2**20)


def cost(macs, nbytes, scale=1):
    return pl.CostEstimate(
        flops=2 * macs // scale, bytes_accessed=nbytes // scale, transcendentals=0
    )


def pinned(weight):
    return pltpu.with_memory_space_constraint(weight, pltpu.HBM)


def row_blocks(d):
    step = step_of(d)
    return [pl.ds(at, step) for at in range(0, d, step)]


def load_kernel(first, gate, up, gate_out, up_out, mark, sems):
    mark[...] = jnp.zeros_like(mark)
    take = pl.ds(first, gate_out.shape[1])
    copies = [
        pltpu.make_async_copy(source.at[part, take], target.at[part], sems.at[which, i])
        for which, (source, target) in enumerate(((gate, gate_out), (up, up_out)))
        for i, part in enumerate(row_blocks(gate.shape[0]))
    ]
    for copy in copies:
        copy.start()
    for copy in copies:
        copy.wait()


def load_part(gate, up, first, width):
    d = gate.shape[0]
    loaded = pl.pallas_call(
        functools.partial(load_kernel, first),
        in_specs=[ANYWHERE] * 2,
        out_specs=[RESIDENT] * 3,
        out_shape=[pltpu.VMEM((d, width), BF16)] * 2 + [jax.ShapeDtypeStruct((8, 128), F32)],
        scratch_shapes=[pltpu.SemaphoreType.DMA((2, len(row_blocks(d))))],
        compiler_params=params(2),
        cost_estimate=cost(0, 4 * d * width),
        name="load_part",
    )(gate, up)
    *values, mark = loaded
    return [pltpu.with_memory_space_constraint(value, pltpu.VMEM) for value in values], mark


def stack_kernel(n, *refs):
    out = refs[-1]
    rows = refs[0].shape[0]
    for i in range(n):
        out[pl.ds(i * rows, rows), :] = refs[i][...]


def stack_part(blocks, after):
    rows, d = blocks[0].shape
    return pl.pallas_call(
        functools.partial(stack_kernel, len(blocks)),
        in_specs=[RESIDENT] * len(blocks) + [ANYWHERE] * len(after),
        out_specs=RESIDENT,
        out_shape=jax.ShapeDtypeStruct((len(blocks) * rows, d), BF16),
        compiler_params=params(12),
        cost_estimate=cost(0, 4 * rows * d, 32),
        name="stack_part",
    )(*blocks, *after)


def join_kernel(own, theirs, out, turned):
    half = own.shape[0]
    core = lax.rem(lax.axis_index("mod"), 2)
    out[pl.ds(pl.multiple_of(core * half, half), half), :] = own[...]
    out[pl.ds(pl.multiple_of((1 - core) * half, half), half), :] = theirs[...]
    turned[...] = out[...].T


def join_part(own, theirs):
    half, d = own.shape
    return pl.pallas_call(
        join_kernel,
        in_specs=[RESIDENT] * 2,
        out_specs=[RESIDENT] * 2,
        out_shape=[
            jax.ShapeDtypeStruct((2 * half, d), BF16),
            jax.ShapeDtypeStruct((d, 2 * half), BF16),
        ],
        compiler_params=params(24),
        cost_estimate=cost(0, 8 * half * d, 32),
        name="join_part",
    )(own, theirs)


def split_rows(value, keep, send, at):
    half = keep.shape[0]
    put = pl.ds(at, value.shape[1])
    keep[:, put] = value[:half]
    send[:, put] = value[half:].astype(BF16)


def first_kernel(tile, has_prev, x, weight, *refs):
    keep, send = refs[-2:]
    width = weight.shape[1]
    if has_prev:
        keep[:, :width] = refs[0][:, :width]
        send[:, :width] = refs[1][:, :width]
    start = width if has_prev else 0
    for at in range(0, width, tile):
        value = lax.dot_general(
            x[...], weight[:, pl.ds(at, tile)], ROWS, preferred_element_type=F32
        )
        split_rows(value, keep, send, start + at)


def piece_shapes(tokens, total):
    return [
        jax.ShapeDtypeStruct((tokens // 2, total), F32),
        jax.ShapeDtypeStruct((tokens // 2, total), BF16),
    ]


def first_part(x, weight, prev, tile, after):
    t, d = x.shape
    width = weight.shape[1]
    return pl.pallas_call(
        functools.partial(first_kernel, tile, len(prev) > 0),
        in_specs=[RESIDENT] * (2 + len(prev)) + [ANYWHERE] * len(after),
        out_specs=[RESIDENT] * 2,
        out_shape=piece_shapes(t, 2 * width),
        compiler_params=params(8),
        cost_estimate=cost(t * d * width, 2 * d * width, 32),
        name="first_part",
    )(x, weight, *prev, *after)


def forward_kernel(jobs, tile, kinds, *refs):
    n = len(kinds)
    rows = dict(zip(sorted({kind for kind, _ in kinds}), refs))
    weights = dict(zip(kinds, refs[len(rows) : len(rows) + n]))
    keep, send, tall, wide, sums, sems = refs[-6:]
    blocks = row_blocks(tall.shape[0])
    steps, start, used = [], 0, 0

    def step(source, target, work):
        steps.append((pltpu.make_async_copy(source, target, sems.at[len(steps)]), work))

    def tall_work(i, part, at, width):
        for col in range(at, at + width, tile):
            put = pl.ds(col, tile)
            value = lax.dot_general(
                rows["x"][:, part], tall[part, put], ROWS, preferred_element_type=F32
            )
            if i:
                value += sums[:, put]
            if i + 1 < len(blocks):
                sums[:, put] = value
            else:
                split_rows(value, keep, send, col)

    def wide_work(target, at):
        value = lax.dot_general(target[...], rows["g"][...], ROWS, preferred_element_type=F32)
        split_rows(value.T, keep, send, at)

    for (kind, name), first, tiles in jobs:
        weight, width = weights[(kind, name)], tiles * tile
        if kind == "x":
            put = pl.ds(start, width)
            for i, part in enumerate(blocks):
                source = weight.at[part, pl.ds(first * tile, width)]
                work = functools.partial(tall_work, i, part, start, width)
                step(source, tall.at[part, put], work)
        else:
            for i in range(tiles):
                source = weight.at[pl.ds((first + i) * tile, tile)]
                target = wide.at[used]
                step(source, target, functools.partial(wide_work, target, start + i * tile))
                used += 1
        start += width
    for copy, _ in steps[:FLIGHT]:
        copy.start()
    for i, (copy, work) in enumerate(steps):
        copy.wait()
        for later, _ in steps[i + FLIGHT : i + FLIGHT + 1]:
            later.start()
        work()


def forward_part(rows, weights, jobs, tile, half, after=()):
    kinds = sorted({key for key, _, _ in jobs})
    used = [rows[kind] for kind in sorted({kind for kind, _ in kinds})]
    d, t = weights[kinds[0]].shape[1 if kinds[0][0] == "g" else 0], 2 * half
    n_wide = sum(tiles for key, _, tiles in jobs if key[0] == "g")
    tall_jobs = [tiles for key, _, tiles in jobs if key[0] == "x"]
    tall_width = max(sum(tall_jobs), 1) * tile
    total = (n_wide + sum(tall_jobs)) * tile
    return pl.pallas_call(
        functools.partial(forward_kernel, jobs, tile, kinds),
        in_specs=[RESIDENT] * len(used) + [ANYWHERE] * (len(kinds) + len(after)),
        out_specs=[RESIDENT] * 2,
        out_shape=piece_shapes(t, total),
        scratch_shapes=[
            pltpu.VMEM((d, tall_width), BF16),
            pltpu.VMEM((max(n_wide, 1), tile, d), BF16),
            pltpu.VMEM((t, tall_width), F32),
            pltpu.SemaphoreType.DMA((n_wide + len(tall_jobs) * len(row_blocks(d)),)),
        ],
        compiler_params=params(28),
        cost_estimate=cost(2 * t * d * total, 2 * d * total, 32),
        name="forward_part",
    )(*used, *[weights[key] for key in kinds], *after)


def step_of(d):
    return 512 if d % 512 == 0 else d


def joined(mine, peer, slot):
    return jnp.concatenate([mine[slot], peer[slot]], axis=0)


def input_kernel(has_prev, first, *refs):
    mine, peer, wg, wu, *others = refs
    prev = others[0]
    out, gate_buf, up_buf, sems = refs[-4:]
    parts = row_blocks(wg.shape[0])
    cols = pl.ds(first, mine.shape[2])
    copies = [
        (
            pltpu.make_async_copy(wg.at[part, cols], gate_buf.at[part], sems.at[0, i]),
            pltpu.make_async_copy(wu.at[part, cols], up_buf.at[part], sems.at[1, i]),
        )
        for i, part in enumerate(parts)
    ]
    for pair in copies[:PAIRS]:
        for copy in pair:
            copy.start()
    gb = joined(mine, peer, 1)
    ub = joined(mine, peer, 2)
    for i, (part, pair) in enumerate(zip(parts, copies)):
        for copy in pair:
            copy.wait()
        for later in copies[i + PAIRS : i + PAIRS + 1]:
            for copy in later:
                copy.start()
        value = lax.dot_general(gb, gate_buf[part, :], COLS, preferred_element_type=F32)
        value += lax.dot_general(ub, up_buf[part, :], COLS, preferred_element_type=F32)
        out[:, part] = value + prev[:, part] if has_prev else value


def input_part(prev, mine, peer, wg, wu, first, after):
    t, d, span = 2 * mine.shape[1], wg.shape[0], mine.shape[2]
    has_prev = prev is not None
    return pl.pallas_call(
        functools.partial(input_kernel, has_prev, first),
        in_specs=[RESIDENT] * 2
        + [ANYWHERE] * 2
        + [RESIDENT] * int(has_prev)
        + [ANYWHERE] * len(after),
        out_specs=RESIDENT,
        out_shape=jax.ShapeDtypeStruct((t, d), F32),
        scratch_shapes=[
            pltpu.VMEM((d, span), BF16),
            pltpu.VMEM((d, span), BF16),
            pltpu.SemaphoreType.DMA((2, len(row_blocks(d)))),
        ],
        compiler_params=params(28),
        cost_estimate=cost(2 * t * d * span, 4 * d * span),
        name="input_part",
    )(mine, peer, wg, wu, *([prev] if has_prev else []), *after)


def weight_kernel(firsts, tile, *refs):
    n = len(firsts)
    xt, g = refs[:2]
    acts = [(refs[2 + 2 * i], refs[3 + 2 * i]) for i in range(n)]
    grad_gate, grad_up, grad_down, gate_buf, up_buf, down_buf, sems = refs[-7:]
    d = xt.shape[0]
    step = step_of(d)
    copies = []

    def out(source, target):
        copy = pltpu.make_async_copy(source, target, sems.at[len(copies)])
        copy.start()
        copies.append(copy)

    start = 0
    for first, (mine, peer) in zip(firsts, acts):
        span = mine.shape[2]
        held, cols = pl.ds(start, span), pl.ds(first, span)
        gb = joined(mine, peer, 1)
        ub = joined(mine, peer, 2)
        ht = joined(mine, peer, 0).T
        for at in range(0, d, step):
            part = pl.ds(at, step)
            rows = xt[part, :]
            for value, buf, grad in ((gb, gate_buf, grad_gate), (ub, up_buf, grad_up)):
                buf[part, held] = lax.dot_general(
                    rows, value, ROWS, preferred_element_type=F32
                ).astype(BF16)
                out(buf.at[part, held], grad.at[part, cols])
        for at in range(0, span, tile):
            part = pl.ds(start + at, tile)
            down_buf[part, :] = lax.dot_general(
                ht[at : at + tile], g[...], ROWS, preferred_element_type=F32
            ).astype(BF16)
            out(down_buf.at[part], grad_down.at[pl.ds(first + at, tile)])
        start += span
    for copy in copies:
        copy.wait()


def weight_part(prev, xt, g, acts, firsts, tile, hidden, after):
    t, d = g.shape
    prev = [] if prev is None else list(prev)
    spans = [mine.shape[2] for mine, _ in acts]
    total = sum(spans)
    n_copies = len(acts) * 2 * (d // step_of(d)) + total // tile
    flat = [array for pair in acts for array in pair]
    return pl.pallas_call(
        functools.partial(weight_kernel, firsts, tile),
        in_specs=[RESIDENT] * (2 + len(flat)) + [ANYWHERE] * (len(prev) + len(after)),
        out_specs=[ANYWHERE] * 3,
        out_shape=[
            jax.ShapeDtypeStruct((d, hidden), BF16),
            jax.ShapeDtypeStruct((d, hidden), BF16),
            jax.ShapeDtypeStruct((hidden, d), BF16),
        ],
        scratch_shapes=[
            pltpu.VMEM((d, total), BF16),
            pltpu.VMEM((d, total), BF16),
            pltpu.VMEM((total, d), BF16),
            pltpu.SemaphoreType.DMA((n_copies,)),
        ],
        input_output_aliases={2 + len(flat) + i: i for i in range(len(prev))},
        compiler_params=params(34),
        cost_estimate=cost(3 * t * d * total, 6 * d * total),
        name="weight_part",
    )(xt, g, *flat, *prev, *after)


def add_kernel(keep, got, *refs):
    refs[-1][...] = (keep[...] + got[...].astype(F32)).astype(BF16)


def add_part(keep, got, after=()):
    return pl.pallas_call(
        add_kernel,
        in_specs=[RESIDENT] * 2 + [ANYWHERE] * len(after),
        out_specs=RESIDENT,
        out_shape=jax.ShapeDtypeStruct(keep.shape, BF16),
        compiler_params=params(16),
        cost_estimate=cost(keep.size, 8 * keep.size, 64),
        name="add_part",
    )(keep, got, *after)


def swiglu_kernel(places, tile, n_sums, *refs):
    out = refs[-1]
    for i, place in enumerate(places):
        gate, up, grad_hidden = (
            refs[which * n_sums][:, pl.ds(first, tile)]
            + sum(
                refs[which * n_sums + j][:, pl.ds(first, tile)].astype(F32)
                for j in range(1, n_sums)
            )
            for which, first in place
        )
        sigmoid_gate = jax.nn.sigmoid(gate)
        active = gate * sigmoid_gate
        slope = sigmoid_gate * (1.0 + gate * (1.0 - sigmoid_gate))
        part = pl.ds(i * tile, tile)
        out[0, :, part] = (active * up).astype(BF16)
        out[1, :, part] = (grad_hidden * up * slope).astype(BF16)
        out[2, :, part] = (grad_hidden * active).astype(BF16)


def swiglu_part(places, pieces, tile, after=()):
    width = len(places) * tile
    flat = [array for piece in pieces for array in piece]
    rows = flat[0].shape[0]
    return pl.pallas_call(
        functools.partial(swiglu_kernel, places, tile, len(pieces[0])),
        in_specs=[RESIDENT] * len(flat) + [ANYWHERE] * len(after),
        out_specs=RESIDENT,
        out_shape=jax.ShapeDtypeStruct((3, rows, width), BF16),
        compiler_params=params(20),
        cost_estimate=cost(20 * rows * width, 14 * rows * width, 64),
        name="swiglu_part",
    )(*flat, *after)


def shards(n_hid, n_mod, tokens, grad_output, gate_weight, up_weight, down_weight):
    hidden = gate_weight.shape[1]
    rows = tokens.shape[0]
    far = n_hid // 2
    core = lax.axis_index("mod") % 2

    def swap(value, axis, size, bit):
        return lax.ppermute(value, axis, [(i ^ bit, i) for i in range(size)])

    def from_far(value, k):
        return swap(value, "hid", n_hid, 2 * k)

    def near(value):
        return swap(value, "hid", n_hid, 1)

    def other_core(value):
        return swap(value, "mod", n_mod, 1)

    def along(block):
        return [block] + [from_far(block, k) for k in range(1, far)]

    def across(column, after):
        own = stack_part(column, after)
        return join_part(own, near(own))

    gate_key, up_key, down_key = ("x", 0), ("x", 1), ("g", 2)
    weights = {
        gate_key: pinned(gate_weight),
        up_key: pinned(up_weight),
        down_key: pinned(down_weight),
    }

    tile = next((n for n in (256, 128) if hidden % n == 0), hidden)
    n_tiles = hidden // tile

    def ranges(edges):
        bounds = [round(e * n_tiles / edges[-1]) for e in edges]
        return list(zip(bounds[:-1], bounds[1:]))

    spans = [(a, b) for a, b in ranges(SPAN_EDGES) if b > a]
    a, b = next((a, b) for a, b in ranges(GATE_EDGES) if b > a)
    loaded, mark = load_part(weights[gate_key], weights[up_key], a * tile, (b - a) * tile)

    x, x_turned = across(along(tokens), [mark])
    column = along(grad_output)
    rows_of = {"x": x}

    def exchanged(jobs, after=()):
        if pieces:
            keep, send = forward_part(rows_of, weights, jobs, tile, rows * far, after)
        else:
            half = first_part(x, loaded[0], [], tile, [])
            keep, send = first_part(x, loaded[1], half, tile, after)
        got = other_core(send)
        narrow = add_part(keep, got, pieces[-1][-1:] if len(pieces) == 3 else ())
        others = [swap(narrow, "mod", n_mod, 2 * k) for k in range(1, n_mod // 2)]
        return (keep, got, *others), send, narrow

    n = len(spans)
    pieces, sends, narrows = [], [], []
    where = {gate_key: [], up_key: [], down_key: []}
    for (a, b), (c, d) in zip(ranges(GATE_EDGES), ranges(DOWN_EDGES)):
        jobs = [(gate_key, a, b - a), (up_key, a, b - a), (down_key, c, d - c)]
        jobs = [job for job in jobs if job[2]]
        if not jobs:
            continue
        k, at = len(pieces), 0
        for key, _, tiles in jobs:
            where[key] += [(k, at + i * tile) for i in range(tiles)]
            at += tiles * tile
        after = narrows[-1:] + [piece[-1] for piece in pieces[-2:-1]]
        after = after if pieces else column[1:]
        for kept, value in zip((pieces, sends, narrows), exchanged(jobs, after)):
            kept.append(value)
        if k == 0:
            g, rows_of["g"] = across(column, sends[:1])

    def act(i, after=()):
        places = list(zip(*(where[key][slice(*spans[i])] for key in (gate_key, up_key, down_key))))
        used = sorted({which for place in places for which, _ in place})
        local = [[(used.index(which), first) for which, first in place] for place in places]
        mine = swiglu_part(local, [pieces[which] for which in used], tile, after)
        return mine, other_core(mine)

    def weight_grads(prev, group, after):
        return weight_part(
            prev,
            x_turned,
            g,
            [acts[j] for j in group],
            [spans[j][0] * tile for j in group],
            tile,
            hidden,
            after,
        )

    def tokens_grad(prev, i, after):
        mine, peer = acts[i]
        first = spans[i][0] * tile
        return input_part(prev, mine, peer, weights[gate_key], weights[up_key], first, after)

    acts = [act(0, narrows[-1:])]
    total = tokens_grad(None, 0, narrows[-1:])
    for i in range(1, n):
        acts.append(act(i, [total]))
    for i in range(1, n):
        total = tokens_grad(total, i, [])

    half = total.shape[0] // 2
    top, bottom = total[:half], total[half:]
    own = jnp.where(core == 0, top, bottom)
    theirs = jnp.where(core == 0, bottom, top).astype(BF16)
    own = own + near(theirs).astype(F32)
    result = own[:rows]
    for k in range(1, far):
        block = own[k * rows : (k + 1) * rows].astype(BF16)
        result = result + from_far(block, k).astype(F32)

    grads = None
    for group in ([0], list(range(1, n))):
        if group:
            grads = weight_grads(grads, group, [theirs])
    grad_gate, grad_up, grad_down = grads
    return (result.astype(BF16), grad_gate, grad_up, grad_down)


def solution(mesh):
    placed = (P("hid", "mod"), P("hid", "mod"), P("mod", "hid"), P("mod", "hid"), P("hid", "mod"))
    return jax.shard_map(
        functools.partial(shards, mesh.shape["hid"], mesh.shape["mod"]),
        mesh=mesh,
        in_specs=placed,
        out_specs=(P("hid", "mod"), P("mod", "hid"), P("mod", "hid"), P("hid", "mod")),
        check_vma=False,
    )
```

```python
import functools

import jax
import jax.numpy as jnp
from jax import lax
from jax.experimental import pallas as pl
from jax.experimental.pallas import tpu as pltpu
from jax.sharding import PartitionSpec as P

F32 = jnp.float32
BF16 = jnp.bfloat16
ROWS = (((1,), (0,)), ((), ()))
COLS = (((1,), (1,)), ((), ()))
GATE_EDGES = (0, 8, 14, 14, 14)
DOWN_EDGES = (0, 0, 0, 8, 14)
SPAN_EDGES = (0, 7, 14)
FLIGHT = 4
PAIRS = 2
ANYWHERE = pl.BlockSpec(memory_space=pl.ANY)
RESIDENT = pl.BlockSpec(memory_space=pltpu.VMEM)


def params(mib):
    return pltpu.CompilerParams(vmem_limit_bytes=mib * 2**20)


def cost(macs, nbytes, scale=1):
    return pl.CostEstimate(
        flops=2 * macs // scale, bytes_accessed=nbytes // scale, transcendentals=0
    )


def pinned(weight):
    return pltpu.with_memory_space_constraint(weight, pltpu.HBM)


def row_blocks(d):
    step = step_of(d)
    return [pl.ds(at, step) for at in range(0, d, step)]


def load_kernel(first, gate, up, gate_out, up_out, mark, sems):
    mark[...] = jnp.zeros_like(mark)
    take = pl.ds(first, gate_out.shape[1])
    copies = [
        pltpu.make_async_copy(source.at[part, take], target.at[part], sems.at[which, i])
        for which, (source, target) in enumerate(((gate, gate_out), (up, up_out)))
        for i, part in enumerate(row_blocks(gate.shape[0]))
    ]
    for copy in copies:
        copy.start()
    for copy in copies:
        copy.wait()


def load_part(gate, up, first, width):
    d = gate.shape[0]
    loaded = pl.pallas_call(
        functools.partial(load_kernel, first),
        in_specs=[ANYWHERE] * 2,
        out_specs=[RESIDENT] * 3,
        out_shape=[pltpu.VMEM((d, width), BF16)] * 2 + [jax.ShapeDtypeStruct((8, 128), F32)],
        scratch_shapes=[pltpu.SemaphoreType.DMA((2, len(row_blocks(d))))],
        compiler_params=params(2),
        cost_estimate=cost(0, 4 * d * width),
        name="load_part",
    )(gate, up)
    *values, mark = loaded
    return [pltpu.with_memory_space_constraint(value, pltpu.VMEM) for value in values], mark


def stack_kernel(n, *refs):
    out = refs[-1]
    rows = refs[0].shape[0]
    for i in range(n):
        out[pl.ds(i * rows, rows), :] = refs[i][...]


def stack_part(blocks, after):
    rows, d = blocks[0].shape
    return pl.pallas_call(
        functools.partial(stack_kernel, len(blocks)),
        in_specs=[RESIDENT] * len(blocks) + [ANYWHERE] * len(after),
        out_specs=RESIDENT,
        out_shape=jax.ShapeDtypeStruct((len(blocks) * rows, d), BF16),
        compiler_params=params(12),
        cost_estimate=cost(0, 4 * rows * d, 32),
        name="stack_part",
    )(*blocks, *after)


def join_kernel(own, theirs, out, turned):
    half = own.shape[0]
    core = lax.rem(lax.axis_index("mod"), 2)
    out[pl.ds(pl.multiple_of(core * half, half), half), :] = own[...]
    out[pl.ds(pl.multiple_of((1 - core) * half, half), half), :] = theirs[...]
    turned[...] = out[...].T


def join_part(own, theirs):
    half, d = own.shape
    return pl.pallas_call(
        join_kernel,
        in_specs=[RESIDENT] * 2,
        out_specs=[RESIDENT] * 2,
        out_shape=[
            jax.ShapeDtypeStruct((2 * half, d), BF16),
            jax.ShapeDtypeStruct((d, 2 * half), BF16),
        ],
        compiler_params=params(24),
        cost_estimate=cost(0, 8 * half * d, 32),
        name="join_part",
    )(own, theirs)


def split_rows(value, keep, send, at):
    half = keep.shape[0]
    put = pl.ds(at, value.shape[1])
    keep[:, put] = value[:half]
    send[:, put] = value[half:].astype(BF16)


def first_kernel(tile, has_prev, x, weight, *refs):
    keep, send = refs[-2:]
    width = weight.shape[1]
    if has_prev:
        keep[:, :width] = refs[0][:, :width]
        send[:, :width] = refs[1][:, :width]
    start = width if has_prev else 0
    for at in range(0, width, tile):
        value = lax.dot_general(
            x[...], weight[:, pl.ds(at, tile)], ROWS, preferred_element_type=F32
        )
        split_rows(value, keep, send, start + at)


def piece_shapes(tokens, total):
    return [
        jax.ShapeDtypeStruct((tokens // 2, total), F32),
        jax.ShapeDtypeStruct((tokens // 2, total), BF16),
    ]


def first_part(x, weight, prev, tile, after):
    t, d = x.shape
    width = weight.shape[1]
    return pl.pallas_call(
        functools.partial(first_kernel, tile, len(prev) > 0),
        in_specs=[RESIDENT] * (2 + len(prev)) + [ANYWHERE] * len(after),
        out_specs=[RESIDENT] * 2,
        out_shape=piece_shapes(t, 2 * width),
        compiler_params=params(8),
        cost_estimate=cost(t * d * width, 2 * d * width, 32),
        name="first_part",
    )(x, weight, *prev, *after)


def forward_kernel(jobs, tile, kinds, *refs):
    n = len(kinds)
    rows = dict(zip(sorted({kind for kind, _ in kinds}), refs))
    weights = dict(zip(kinds, refs[len(rows) : len(rows) + n]))
    keep, send, tall, wide, sums, sems = refs[-6:]
    blocks = row_blocks(tall.shape[0])
    steps, start, used = [], 0, 0

    def step(source, target, work):
        steps.append((pltpu.make_async_copy(source, target, sems.at[len(steps)]), work))

    def tall_work(i, part, at, width):
        for col in range(at, at + width, tile):
            put = pl.ds(col, tile)
            value = lax.dot_general(
                rows["x"][:, part], tall[part, put], ROWS, preferred_element_type=F32
            )
            if i:
                value += sums[:, put]
            if i + 1 < len(blocks):
                sums[:, put] = value
            else:
                split_rows(value, keep, send, col)

    def wide_work(target, at):
        value = lax.dot_general(target[...], rows["g"][...], ROWS, preferred_element_type=F32)
        split_rows(value.T, keep, send, at)

    for (kind, name), first, tiles in jobs:
        weight, width = weights[(kind, name)], tiles * tile
        if kind == "x":
            put = pl.ds(start, width)
            for i, part in enumerate(blocks):
                source = weight.at[part, pl.ds(first * tile, width)]
                work = functools.partial(tall_work, i, part, start, width)
                step(source, tall.at[part, put], work)
        else:
            for i in range(tiles):
                source = weight.at[pl.ds((first + i) * tile, tile)]
                target = wide.at[used]
                step(source, target, functools.partial(wide_work, target, start + i * tile))
                used += 1
        start += width
    for copy, _ in steps[:FLIGHT]:
        copy.start()
    for i, (copy, work) in enumerate(steps):
        copy.wait()
        for later, _ in steps[i + FLIGHT : i + FLIGHT + 1]:
            later.start()
        work()


def forward_part(rows, weights, jobs, tile, half, after=()):
    kinds = sorted({key for key, _, _ in jobs})
    used = [rows[kind] for kind in sorted({kind for kind, _ in kinds})]
    d, t = weights[kinds[0]].shape[1 if kinds[0][0] == "g" else 0], 2 * half
    n_wide = sum(tiles for key, _, tiles in jobs if key[0] == "g")
    tall_jobs = [tiles for key, _, tiles in jobs if key[0] == "x"]
    tall_width = max(sum(tall_jobs), 1) * tile
    total = (n_wide + sum(tall_jobs)) * tile
    return pl.pallas_call(
        functools.partial(forward_kernel, jobs, tile, kinds),
        in_specs=[RESIDENT] * len(used) + [ANYWHERE] * (len(kinds) + len(after)),
        out_specs=[RESIDENT] * 2,
        out_shape=piece_shapes(t, total),
        scratch_shapes=[
            pltpu.VMEM((d, tall_width), BF16),
            pltpu.VMEM((max(n_wide, 1), tile, d), BF16),
            pltpu.VMEM((t, tall_width), F32),
            pltpu.SemaphoreType.DMA((n_wide + len(tall_jobs) * len(row_blocks(d)),)),
        ],
        compiler_params=params(28),
        cost_estimate=cost(2 * t * d * total, 2 * d * total, 32),
        name="forward_part",
    )(*used, *[weights[key] for key in kinds], *after)


def step_of(d):
    return 512 if d % 512 == 0 else d


def joined(mine, peer, slot):
    return jnp.concatenate([mine[slot], peer[slot]], axis=0)


def input_kernel(has_prev, first, *refs):
    mine, peer, wg, wu, *others = refs
    prev = others[0]
    out, gate_buf, up_buf, sems = refs[-4:]
    parts = row_blocks(wg.shape[0])
    cols = pl.ds(first, mine.shape[2])
    copies = [
        (
            pltpu.make_async_copy(wg.at[part, cols], gate_buf.at[part], sems.at[0, i]),
            pltpu.make_async_copy(wu.at[part, cols], up_buf.at[part], sems.at[1, i]),
        )
        for i, part in enumerate(parts)
    ]
    for pair in copies[:PAIRS]:
        for copy in pair:
            copy.start()
    gb = joined(mine, peer, 1)
    ub = joined(mine, peer, 2)
    for i, (part, pair) in enumerate(zip(parts, copies)):
        for copy in pair:
            copy.wait()
        for later in copies[i + PAIRS : i + PAIRS + 1]:
            for copy in later:
                copy.start()
        value = lax.dot_general(gb, gate_buf[part, :], COLS, preferred_element_type=F32)
        value += lax.dot_general(ub, up_buf[part, :], COLS, preferred_element_type=F32)
        out[:, part] = value + prev[:, part] if has_prev else value


def input_part(prev, mine, peer, wg, wu, first, after):
    t, d, span = 2 * mine.shape[1], wg.shape[0], mine.shape[2]
    has_prev = prev is not None
    return pl.pallas_call(
        functools.partial(input_kernel, has_prev, first),
        in_specs=[RESIDENT] * 2
        + [ANYWHERE] * 2
        + [RESIDENT] * int(has_prev)
        + [ANYWHERE] * len(after),
        out_specs=RESIDENT,
        out_shape=jax.ShapeDtypeStruct((t, d), F32),
        scratch_shapes=[
            pltpu.VMEM((d, span), BF16),
            pltpu.VMEM((d, span), BF16),
            pltpu.SemaphoreType.DMA((2, len(row_blocks(d)))),
        ],
        compiler_params=params(28),
        cost_estimate=cost(2 * t * d * span, 4 * d * span),
        name="input_part",
    )(mine, peer, wg, wu, *([prev] if has_prev else []), *after)


def weight_kernel(firsts, tile, *refs):
    n = len(firsts)
    xt, g = refs[:2]
    acts = [(refs[2 + 2 * i], refs[3 + 2 * i]) for i in range(n)]
    grad_gate, grad_up, grad_down, gate_buf, up_buf, down_buf, sems = refs[-7:]
    d = xt.shape[0]
    step = step_of(d)
    copies = []

    def out(source, target):
        copy = pltpu.make_async_copy(source, target, sems.at[len(copies)])
        copy.start()
        copies.append(copy)

    start = 0
    for first, (mine, peer) in zip(firsts, acts):
        span = mine.shape[2]
        held, cols = pl.ds(start, span), pl.ds(first, span)
        gb = joined(mine, peer, 1)
        ub = joined(mine, peer, 2)
        ht = joined(mine, peer, 0).T
        for at in range(0, d, step):
            part = pl.ds(at, step)
            rows = xt[part, :]
            for value, buf, grad in ((gb, gate_buf, grad_gate), (ub, up_buf, grad_up)):
                buf[part, held] = lax.dot_general(
                    rows, value, ROWS, preferred_element_type=F32
                ).astype(BF16)
                out(buf.at[part, held], grad.at[part, cols])
        for at in range(0, span, tile):
            part = pl.ds(start + at, tile)
            down_buf[part, :] = lax.dot_general(
                ht[at : at + tile], g[...], ROWS, preferred_element_type=F32
            ).astype(BF16)
            out(down_buf.at[part], grad_down.at[pl.ds(first + at, tile)])
        start += span
    for copy in copies:
        copy.wait()


def weight_part(prev, xt, g, acts, firsts, tile, hidden, after):
    t, d = g.shape
    prev = [] if prev is None else list(prev)
    spans = [mine.shape[2] for mine, _ in acts]
    total = sum(spans)
    n_copies = len(acts) * 2 * (d // step_of(d)) + total // tile
    flat = [array for pair in acts for array in pair]
    return pl.pallas_call(
        functools.partial(weight_kernel, firsts, tile),
        in_specs=[RESIDENT] * (2 + len(flat)) + [ANYWHERE] * (len(prev) + len(after)),
        out_specs=[ANYWHERE] * 3,
        out_shape=[
            jax.ShapeDtypeStruct((d, hidden), BF16),
            jax.ShapeDtypeStruct((d, hidden), BF16),
            jax.ShapeDtypeStruct((hidden, d), BF16),
        ],
        scratch_shapes=[
            pltpu.VMEM((d, total), BF16),
            pltpu.VMEM((d, total), BF16),
            pltpu.VMEM((total, d), BF16),
            pltpu.SemaphoreType.DMA((n_copies,)),
        ],
        input_output_aliases={2 + len(flat) + i: i for i in range(len(prev))},
        compiler_params=params(34),
        cost_estimate=cost(3 * t * d * total, 6 * d * total),
        name="weight_part",
    )(xt, g, *flat, *prev, *after)


def add_kernel(keep, got, *refs):
    refs[-1][...] = (keep[...] + got[...].astype(F32)).astype(BF16)


def add_part(keep, got, after=()):
    return pl.pallas_call(
        add_kernel,
        in_specs=[RESIDENT] * 2 + [ANYWHERE] * len(after),
        out_specs=RESIDENT,
        out_shape=jax.ShapeDtypeStruct(keep.shape, BF16),
        compiler_params=params(16),
        cost_estimate=cost(keep.size, 8 * keep.size, 64),
        name="add_part",
    )(keep, got, *after)


def swiglu_kernel(places, tile, n_sums, *refs):
    out = refs[-1]
    for i, place in enumerate(places):
        gate, up, grad_hidden = (
            refs[which * n_sums][:, pl.ds(first, tile)]
            + sum(
                refs[which * n_sums + j][:, pl.ds(first, tile)].astype(F32)
                for j in range(1, n_sums)
            )
            for which, first in place
        )
        sigmoid_gate = jax.nn.sigmoid(gate)
        active = gate * sigmoid_gate
        slope = sigmoid_gate * (1.0 + gate * (1.0 - sigmoid_gate))
        part = pl.ds(i * tile, tile)
        out[0, :, part] = (active * up).astype(BF16)
        out[1, :, part] = (grad_hidden * up * slope).astype(BF16)
        out[2, :, part] = (grad_hidden * active).astype(BF16)


def swiglu_part(places, pieces, tile, after=()):
    width = len(places) * tile
    flat = [array for piece in pieces for array in piece]
    rows = flat[0].shape[0]
    return pl.pallas_call(
        functools.partial(swiglu_kernel, places, tile, len(pieces[0])),
        in_specs=[RESIDENT] * len(flat) + [ANYWHERE] * len(after),
        out_specs=RESIDENT,
        out_shape=jax.ShapeDtypeStruct((3, rows, width), BF16),
        compiler_params=params(20),
        cost_estimate=cost(20 * rows * width, 14 * rows * width, 64),
        name="swiglu_part",
    )(*flat, *after)


def shards(n_hid, n_mod, tokens, grad_output, gate_weight, up_weight, down_weight):
    hidden = gate_weight.shape[1]
    rows = tokens.shape[0]
    far = n_hid // 2
    core = lax.axis_index("mod") % 2

    def swap(value, axis, size, bit):
        return lax.ppermute(value, axis, [(i ^ bit, i) for i in range(size)])

    def from_far(value, k):
        return swap(value, "hid", n_hid, 2 * k)

    def near(value):
        return swap(value, "hid", n_hid, 1)

    def other_core(value):
        return swap(value, "mod", n_mod, 1)

    def along(block):
        return [block] + [from_far(block, k) for k in range(1, far)]

    def across(column, after):
        own = stack_part(column, after)
        return join_part(own, near(own))

    gate_key, up_key, down_key = ("x", 0), ("x", 1), ("g", 2)
    weights = {
        gate_key: pinned(gate_weight),
        up_key: pinned(up_weight),
        down_key: pinned(down_weight),
    }

    tile = next((n for n in (256, 128) if hidden % n == 0), hidden)
    n_tiles = hidden // tile

    def ranges(edges):
        bounds = [round(e * n_tiles / edges[-1]) for e in edges]
        return list(zip(bounds[:-1], bounds[1:]))

    spans = [(a, b) for a, b in ranges(SPAN_EDGES) if b > a]
    a, b = next((a, b) for a, b in ranges(GATE_EDGES) if b > a)
    loaded, mark = load_part(weights[gate_key], weights[up_key], a * tile, (b - a) * tile)

    x, x_turned = across(along(tokens), [mark])
    column = along(grad_output)
    rows_of = {"x": x}

    def exchanged(jobs, after=()):
        if pieces:
            keep, send = forward_part(rows_of, weights, jobs, tile, rows * far, after)
        else:
            half = first_part(x, loaded[0], [], tile, [])
            keep, send = first_part(x, loaded[1], half, tile, after)
        got = other_core(send)
        narrow = add_part(keep, got, pieces[-1][-1:] if len(pieces) == 3 else ())
        others = [swap(narrow, "mod", n_mod, 2 * k) for k in range(1, n_mod // 2)]
        return (keep, got, *others), send, narrow

    n = len(spans)
    pieces, sends, narrows = [], [], []
    where = {gate_key: [], up_key: [], down_key: []}
    for (a, b), (c, d) in zip(ranges(GATE_EDGES), ranges(DOWN_EDGES)):
        jobs = [(gate_key, a, b - a), (up_key, a, b - a), (down_key, c, d - c)]
        jobs = [job for job in jobs if job[2]]
        if not jobs:
            continue
        k, at = len(pieces), 0
        for key, _, tiles in jobs:
            where[key] += [(k, at + i * tile) for i in range(tiles)]
            at += tiles * tile
        after = narrows[-1:] + [piece[-1] for piece in pieces[-2:-1]]
        after = after if pieces else column[1:]
        for kept, value in zip((pieces, sends, narrows), exchanged(jobs, after)):
            kept.append(value)
        if k == 0:
            g, rows_of["g"] = across(column, sends[:1])

    def act(i, after=()):
        places = list(zip(*(where[key][slice(*spans[i])] for key in (gate_key, up_key, down_key))))
        used = sorted({which for place in places for which, _ in place})
        local = [[(used.index(which), first) for which, first in place] for place in places]
        mine = swiglu_part(local, [pieces[which] for which in used], tile, after)
        return mine, other_core(mine)

    def weight_grads(prev, group, after):
        return weight_part(
            prev,
            x_turned,
            g,
            [acts[j] for j in group],
            [spans[j][0] * tile for j in group],
            tile,
            hidden,
            after,
        )

    def tokens_grad(prev, i, after):
        mine, peer = acts[i]
        first = spans[i][0] * tile
        return input_part(prev, mine, peer, weights[gate_key], weights[up_key], first, after)

    acts = [act(0, narrows[-1:])]
    total = tokens_grad(None, 0, narrows[-1:])
    for i in range(1, n):
        acts.append(act(i, [total]))
    for i in range(1, n):
        total = tokens_grad(total, i, [])

    half = total.shape[0] // 2
    top, bottom = total[:half], total[half:]
    own = jnp.where(core == 0, top, bottom)
    theirs = jnp.where(core == 0, bottom, top).astype(BF16)
    own = own + near(theirs).astype(F32)
    result = own[:rows]
    for k in range(1, far):
        block = own[k * rows : (k + 1) * rows].astype(BF16)
        result = result + from_far(block, k).astype(F32)

    grads = None
    for group in ([0], list(range(1, n))):
        if group:
            grads = weight_grads(grads, group, [theirs])
    grad_gate, grad_up, grad_down = grads
    return (result.astype(BF16), grad_gate, grad_up, grad_down)


def solution(mesh):
    placed = (P("hid", "mod"), P("hid", "mod"), P("mod", "hid"), P("mod", "hid"), P("hid", "mod"))
    return jax.shard_map(
        functools.partial(shards, mesh.shape["hid"], mesh.shape["mod"]),
        mesh=mesh,
        in_specs=placed,
        out_specs=(P("hid", "mod"), P("mod", "hid"), P("mod", "hid"), P("hid", "mod")),
        check_vma=False,
    )
```

```python
import functools

import jax
import jax.numpy as jnp
from jax import lax
from jax.experimental import pallas as pl
from jax.experimental.pallas import tpu as pltpu
from jax.sharding import PartitionSpec as P

F32 = jnp.float32
BF16 = jnp.bfloat16
ROWS = (((1,), (0,)), ((), ()))
COLS = (((1,), (1,)), ((), ()))
GATE_EDGES = (0, 8, 14, 14, 14)
DOWN_EDGES = (0, 0, 0, 8, 14)
SPAN_EDGES = (0, 7, 14)
FLIGHT = 4
PAIRS = 2
ANYWHERE = pl.BlockSpec(memory_space=pl.ANY)
RESIDENT = pl.BlockSpec(memory_space=pltpu.VMEM)


def params(mib):
    return pltpu.CompilerParams(vmem_limit_bytes=mib * 2**20)


def cost(macs, nbytes, scale=1):
    return pl.CostEstimate(
        flops=2 * macs // scale, bytes_accessed=nbytes // scale, transcendentals=0
    )


def pinned(weight):
    return pltpu.with_memory_space_constraint(weight, pltpu.HBM)


def row_blocks(d):
    step = step_of(d)
    return [pl.ds(at, step) for at in range(0, d, step)]


def early_blocks(d):
    step = step_of(d)
    half = step // 2
    return [pl.ds(0, half), pl.ds(half, half)] + row_blocks(d)[1:]


def load_kernel(first, gate, up, gate_out, up_out, mark, sems):
    mark[...] = jnp.zeros_like(mark)
    take = pl.ds(first, gate_out.shape[1])
    copies = [
        pltpu.make_async_copy(source.at[part, take], target.at[part], sems.at[which, i])
        for which, (source, target) in enumerate(((gate, gate_out), (up, up_out)))
        for i, part in enumerate(row_blocks(gate.shape[0]))
    ]
    for copy in copies:
        copy.start()
    for copy in copies:
        copy.wait()


def load_part(gate, up, first, width):
    d = gate.shape[0]
    loaded = pl.pallas_call(
        functools.partial(load_kernel, first),
        in_specs=[ANYWHERE] * 2,
        out_specs=[RESIDENT] * 3,
        out_shape=[pltpu.VMEM((d, width), BF16)] * 2 + [jax.ShapeDtypeStruct((8, 128), F32)],
        scratch_shapes=[pltpu.SemaphoreType.DMA((2, len(row_blocks(d))))],
        compiler_params=params(2),
        cost_estimate=cost(0, 4 * d * width),
        name="load_part",
    )(gate, up)
    *values, mark = loaded
    return [pltpu.with_memory_space_constraint(value, pltpu.VMEM) for value in values], mark


def stack_kernel(n, *refs):
    out = refs[-1]
    rows = refs[0].shape[0]
    for i in range(n):
        out[pl.ds(i * rows, rows), :] = refs[i][...]


def stack_part(blocks, after):
    rows, d = blocks[0].shape
    return pl.pallas_call(
        functools.partial(stack_kernel, len(blocks)),
        in_specs=[RESIDENT] * len(blocks) + [ANYWHERE] * len(after),
        out_specs=RESIDENT,
        out_shape=jax.ShapeDtypeStruct((len(blocks) * rows, d), BF16),
        compiler_params=params(12),
        cost_estimate=cost(0, 4 * rows * d, 32),
        name="stack_part",
    )(*blocks, *after)


def join_kernel(own, theirs, out, turned):
    half = own.shape[0]
    core = lax.rem(lax.axis_index("mod"), 2)
    out[pl.ds(pl.multiple_of(core * half, half), half), :] = own[...]
    out[pl.ds(pl.multiple_of((1 - core) * half, half), half), :] = theirs[...]
    turned[...] = out[...].T


def join_part(own, theirs):
    half, d = own.shape
    return pl.pallas_call(
        join_kernel,
        in_specs=[RESIDENT] * 2,
        out_specs=[RESIDENT] * 2,
        out_shape=[
            jax.ShapeDtypeStruct((2 * half, d), BF16),
            jax.ShapeDtypeStruct((d, 2 * half), BF16),
        ],
        compiler_params=params(24),
        cost_estimate=cost(0, 8 * half * d, 32),
        name="join_part",
    )(own, theirs)


def split_rows(value, keep, send, at):
    half = keep.shape[0]
    put = pl.ds(at, value.shape[1])
    keep[:, put] = value[:half]
    send[:, put] = value[half:].astype(BF16)


def first_kernel(tile, has_prev, x, weight, *refs):
    keep, send = refs[-2:]
    width = weight.shape[1]
    if has_prev:
        keep[:, :width] = refs[0][:, :width]
        send[:, :width] = refs[1][:, :width]
    start = width if has_prev else 0
    for at in range(0, width, tile):
        value = lax.dot_general(
            x[...], weight[:, pl.ds(at, tile)], ROWS, preferred_element_type=F32
        )
        split_rows(value, keep, send, start + at)


def piece_shapes(tokens, total):
    return [
        jax.ShapeDtypeStruct((tokens // 2, total), F32),
        jax.ShapeDtypeStruct((tokens // 2, total), BF16),
    ]


def first_part(x, weight, prev, tile, after):
    t, d = x.shape
    width = weight.shape[1]
    return pl.pallas_call(
        functools.partial(first_kernel, tile, len(prev) > 0),
        in_specs=[RESIDENT] * (2 + len(prev)) + [ANYWHERE] * len(after),
        out_specs=[RESIDENT] * 2,
        out_shape=piece_shapes(t, 2 * width),
        compiler_params=params(8),
        cost_estimate=cost(t * d * width, 2 * d * width, 32),
        name="first_part",
    )(x, weight, *prev, *after)


def forward_kernel(jobs, tile, kinds, *refs):
    n = len(kinds)
    rows = dict(zip(sorted({kind for kind, _ in kinds}), refs))
    weights = dict(zip(kinds, refs[len(rows) : len(rows) + n]))
    keep, send, tall, wide, sums, sems = refs[-6:]
    blocks = row_blocks(tall.shape[0])
    steps, start, used = [], 0, 0

    def step(source, target, work):
        steps.append((pltpu.make_async_copy(source, target, sems.at[len(steps)]), work))

    def tall_work(i, part, at, width):
        for col in range(at, at + width, tile):
            put = pl.ds(col, tile)
            value = lax.dot_general(
                rows["x"][:, part], tall[part, put], ROWS, preferred_element_type=F32
            )
            if i:
                value += sums[:, put]
            if i + 1 < len(blocks):
                sums[:, put] = value
            else:
                split_rows(value, keep, send, col)

    def wide_work(target, at):
        value = lax.dot_general(target[...], rows["g"][...], ROWS, preferred_element_type=F32)
        split_rows(value.T, keep, send, at)

    for (kind, name), first, tiles in jobs:
        weight, width = weights[(kind, name)], tiles * tile
        if kind == "x":
            put = pl.ds(start, width)
            for i, part in enumerate(blocks):
                source = weight.at[part, pl.ds(first * tile, width)]
                work = functools.partial(tall_work, i, part, start, width)
                step(source, tall.at[part, put], work)
        else:
            for i in range(tiles):
                source = weight.at[pl.ds((first + i) * tile, tile)]
                target = wide.at[used]
                step(source, target, functools.partial(wide_work, target, start + i * tile))
                used += 1
        start += width
    for copy, _ in steps[:FLIGHT]:
        copy.start()
    for i, (copy, work) in enumerate(steps):
        copy.wait()
        for later, _ in steps[i + FLIGHT : i + FLIGHT + 1]:
            later.start()
        work()


def forward_part(rows, weights, jobs, tile, half, after=()):
    kinds = sorted({key for key, _, _ in jobs})
    used = [rows[kind] for kind in sorted({kind for kind, _ in kinds})]
    d, t = weights[kinds[0]].shape[1 if kinds[0][0] == "g" else 0], 2 * half
    n_wide = sum(tiles for key, _, tiles in jobs if key[0] == "g")
    tall_jobs = [tiles for key, _, tiles in jobs if key[0] == "x"]
    tall_width = max(sum(tall_jobs), 1) * tile
    total = (n_wide + sum(tall_jobs)) * tile
    return pl.pallas_call(
        functools.partial(forward_kernel, jobs, tile, kinds),
        in_specs=[RESIDENT] * len(used) + [ANYWHERE] * (len(kinds) + len(after)),
        out_specs=[RESIDENT] * 2,
        out_shape=piece_shapes(t, total),
        scratch_shapes=[
            pltpu.VMEM((d, tall_width), BF16),
            pltpu.VMEM((max(n_wide, 1), tile, d), BF16),
            pltpu.VMEM((t, tall_width), F32),
            pltpu.SemaphoreType.DMA((n_wide + len(tall_jobs) * len(row_blocks(d)),)),
        ],
        compiler_params=params(20 if t <= 256 else 32),
        cost_estimate=cost(2 * t * d * total, 2 * d * total, 32),
        name="forward_part",
    )(*used, *[weights[key] for key in kinds], *after)


def step_of(d):
    return 512 if d % 512 == 0 else d


def joined(mine, peer, slot):
    return jnp.concatenate([mine[slot], peer[slot]], axis=0)


def input_kernel(has_prev, first, *refs):
    mine, peer, wg, wu, *others = refs
    prev = others[0]
    out, gate_buf, up_buf, sems = refs[-4:]
    parts = early_blocks(wg.shape[0])
    cols = pl.ds(first, mine.shape[2])
    copies = [
        (
            pltpu.make_async_copy(wg.at[part, cols], gate_buf.at[part], sems.at[0, i]),
            pltpu.make_async_copy(wu.at[part, cols], up_buf.at[part], sems.at[1, i]),
        )
        for i, part in enumerate(parts)
    ]
    for pair in copies[:PAIRS]:
        for copy in pair:
            copy.start()
    gb = joined(mine, peer, 1)
    ub = joined(mine, peer, 2)
    for i, (part, pair) in enumerate(zip(parts, copies)):
        for copy in pair:
            copy.wait()
        for later in copies[i + PAIRS : i + PAIRS + 1]:
            for copy in later:
                copy.start()
        value = lax.dot_general(gb, gate_buf[part, :], COLS, preferred_element_type=F32)
        value += lax.dot_general(ub, up_buf[part, :], COLS, preferred_element_type=F32)
        out[:, part] = value + prev[:, part] if has_prev else value


def input_part(prev, mine, peer, wg, wu, first, after):
    t, d, span = 2 * mine.shape[1], wg.shape[0], mine.shape[2]
    has_prev = prev is not None
    return pl.pallas_call(
        functools.partial(input_kernel, has_prev, first),
        in_specs=[RESIDENT] * 2
        + [ANYWHERE] * 2
        + [RESIDENT] * int(has_prev)
        + [ANYWHERE] * len(after),
        out_specs=RESIDENT,
        out_shape=jax.ShapeDtypeStruct((t, d), F32),
        scratch_shapes=[
            pltpu.VMEM((d, span), BF16),
            pltpu.VMEM((d, span), BF16),
            pltpu.SemaphoreType.DMA((2, len(early_blocks(d)))),
        ],
        compiler_params=params(24 if t <= 256 else 32),
        cost_estimate=cost(2 * t * d * span, 4 * d * span),
        name="input_part",
    )(mine, peer, wg, wu, *([prev] if has_prev else []), *after)


def weight_kernel(firsts, tile, *refs):
    n = len(firsts)
    xt, g = refs[:2]
    acts = [(refs[2 + 2 * i], refs[3 + 2 * i]) for i in range(n)]
    grad_gate, grad_up, grad_down, gate_buf, up_buf, down_buf, sems = refs[-7:]
    d = xt.shape[0]
    step = step_of(d)
    copies = []

    def out(source, target):
        copy = pltpu.make_async_copy(source, target, sems.at[len(copies)])
        copy.start()
        copies.append(copy)

    start = 0
    for first, (mine, peer) in zip(firsts, acts):
        span = mine.shape[2]
        held, cols = pl.ds(start, span), pl.ds(first, span)
        gb = joined(mine, peer, 1)
        ub = joined(mine, peer, 2)
        ht = joined(mine, peer, 0).T
        for at in range(0, d, step):
            part = pl.ds(at, step)
            rows = xt[part, :]
            for value, buf, grad in ((gb, gate_buf, grad_gate), (ub, up_buf, grad_up)):
                buf[part, held] = lax.dot_general(
                    rows, value, ROWS, preferred_element_type=F32
                ).astype(BF16)
                out(buf.at[part, held], grad.at[part, cols])
        for at in range(0, span, tile):
            part = pl.ds(start + at, tile)
            down_buf[part, :] = lax.dot_general(
                ht[at : at + tile], g[...], ROWS, preferred_element_type=F32
            ).astype(BF16)
            out(down_buf.at[part], grad_down.at[pl.ds(first + at, tile)])
        start += span
    for copy in copies:
        copy.wait()


def weight_part(prev, xt, g, acts, firsts, tile, hidden, after):
    t, d = g.shape
    prev = [] if prev is None else list(prev)
    spans = [mine.shape[2] for mine, _ in acts]
    total = sum(spans)
    n_copies = len(acts) * 2 * (d // step_of(d)) + total // tile
    flat = [array for pair in acts for array in pair]
    return pl.pallas_call(
        functools.partial(weight_kernel, firsts, tile),
        in_specs=[RESIDENT] * (2 + len(flat)) + [ANYWHERE] * (len(prev) + len(after)),
        out_specs=[ANYWHERE] * 3,
        out_shape=[
            jax.ShapeDtypeStruct((d, hidden), BF16),
            jax.ShapeDtypeStruct((d, hidden), BF16),
            jax.ShapeDtypeStruct((hidden, d), BF16),
        ],
        scratch_shapes=[
            pltpu.VMEM((d, total), BF16),
            pltpu.VMEM((d, total), BF16),
            pltpu.VMEM((total, d), BF16),
            pltpu.SemaphoreType.DMA((n_copies,)),
        ],
        input_output_aliases={2 + len(flat) + i: i for i in range(len(prev))},
        compiler_params=params(34),
        cost_estimate=cost(3 * t * d * total, 6 * d * total),
        name="weight_part",
    )(xt, g, *flat, *prev, *after)


def add_kernel(keep, got, *refs):
    refs[-1][...] = (keep[...] + got[...].astype(F32)).astype(BF16)


def add_part(keep, got, after=()):
    return pl.pallas_call(
        add_kernel,
        in_specs=[RESIDENT] * 2 + [ANYWHERE] * len(after),
        out_specs=RESIDENT,
        out_shape=jax.ShapeDtypeStruct(keep.shape, BF16),
        compiler_params=params(16),
        cost_estimate=cost(keep.size, 8 * keep.size, 64),
        name="add_part",
    )(keep, got, *after)


def swiglu_kernel(places, tile, n_sums, *refs):
    out = refs[-1]
    for i, place in enumerate(places):
        gate, up, grad_hidden = (
            refs[which * n_sums][:, pl.ds(first, tile)]
            + sum(
                refs[which * n_sums + j][:, pl.ds(first, tile)].astype(F32)
                for j in range(1, n_sums)
            )
            for which, first in place
        )
        sigmoid_gate = jax.nn.sigmoid(gate)
        active = gate * sigmoid_gate
        slope = sigmoid_gate * (1.0 + gate * (1.0 - sigmoid_gate))
        part = pl.ds(i * tile, tile)
        out[0, :, part] = (active * up).astype(BF16)
        out[1, :, part] = (grad_hidden * up * slope).astype(BF16)
        out[2, :, part] = (grad_hidden * active).astype(BF16)


def swiglu_part(places, pieces, tile, after=()):
    width = len(places) * tile
    flat = [array for piece in pieces for array in piece]
    rows = flat[0].shape[0]
    return pl.pallas_call(
        functools.partial(swiglu_kernel, places, tile, len(pieces[0])),
        in_specs=[RESIDENT] * len(flat) + [ANYWHERE] * len(after),
        out_specs=RESIDENT,
        out_shape=jax.ShapeDtypeStruct((3, rows, width), BF16),
        compiler_params=params(20),
        cost_estimate=cost(20 * rows * width, 14 * rows * width, 64),
        name="swiglu_part",
    )(*flat, *after)


def shards(n_hid, n_mod, tokens, grad_output, gate_weight, up_weight, down_weight):
    hidden = gate_weight.shape[1]
    rows = tokens.shape[0]
    far = n_hid // 2
    core = lax.axis_index("mod") % 2

    def swap(value, axis, size, bit):
        return lax.ppermute(value, axis, [(i ^ bit, i) for i in range(size)])

    def from_far(value, k):
        return swap(value, "hid", n_hid, 2 * k)

    def near(value):
        return swap(value, "hid", n_hid, 1)

    def other_core(value):
        return swap(value, "mod", n_mod, 1)

    def along(block):
        return [block] + [from_far(block, k) for k in range(1, far)]

    def across(column, after):
        own = stack_part(column, after)
        return join_part(own, near(own))

    gate_key, up_key, down_key = ("x", 0), ("x", 1), ("g", 2)
    weights = {
        gate_key: pinned(gate_weight),
        up_key: pinned(up_weight),
        down_key: pinned(down_weight),
    }

    tile = next((n for n in (256, 128) if hidden % n == 0), hidden)
    n_tiles = hidden // tile

    def ranges(edges):
        bounds = [round(e * n_tiles / edges[-1]) for e in edges]
        return list(zip(bounds[:-1], bounds[1:]))

    spans = [(a, b) for a, b in ranges(SPAN_EDGES) if b > a]
    a, b = next((a, b) for a, b in ranges(GATE_EDGES) if b > a)
    loaded, mark = load_part(weights[gate_key], weights[up_key], a * tile, (b - a) * tile)

    x, x_turned = across(along(tokens), [mark])
    column = along(grad_output)
    rows_of = {"x": x}

    def exchanged(jobs, after=()):
        if pieces:
            keep, send = forward_part(rows_of, weights, jobs, tile, rows * far, after)
        else:
            half = first_part(x, loaded[0], [], tile, [])
            keep, send = first_part(x, loaded[1], half, tile, after)
        got = other_core(send)
        narrow = add_part(keep, got, pieces[-1][-1:] if len(pieces) == 3 else ())
        others = [swap(narrow, "mod", n_mod, 2 * k) for k in range(1, n_mod // 2)]
        return (keep, got, *others), send, narrow

    n = len(spans)
    pieces, sends, narrows = [], [], []
    where = {gate_key: [], up_key: [], down_key: []}
    for (a, b), (c, d) in zip(ranges(GATE_EDGES), ranges(DOWN_EDGES)):
        jobs = [(gate_key, a, b - a), (up_key, a, b - a), (down_key, c, d - c)]
        jobs = [job for job in jobs if job[2]]
        if not jobs:
            continue
        k, at = len(pieces), 0
        for key, _, tiles in jobs:
            where[key] += [(k, at + i * tile) for i in range(tiles)]
            at += tiles * tile
        after = narrows[-1:] + [piece[-1] for piece in pieces[-2:-1]]
        after = after if pieces else column[1:]
        for kept, value in zip((pieces, sends, narrows), exchanged(jobs, after)):
            kept.append(value)
        if k == 0:
            g, rows_of["g"] = across(column, sends[:1])

    def act(i, after=()):
        places = list(zip(*(where[key][slice(*spans[i])] for key in (gate_key, up_key, down_key))))
        used = sorted({which for place in places for which, _ in place})
        local = [[(used.index(which), first) for which, first in place] for place in places]
        mine = swiglu_part(local, [pieces[which] for which in used], tile, after)
        return mine, other_core(mine)

    def weight_grads(prev, group, after):
        return weight_part(
            prev,
            x_turned,
            g,
            [acts[j] for j in group],
            [spans[j][0] * tile for j in group],
            tile,
            hidden,
            after,
        )

    def tokens_grad(prev, i, after):
        mine, peer = acts[i]
        first = spans[i][0] * tile
        return input_part(prev, mine, peer, weights[gate_key], weights[up_key], first, after)

    acts = [act(0, narrows[-1:])]
    total = tokens_grad(None, 0, narrows[-1:])
    for i in range(1, n):
        acts.append(act(i, [total]))
    for i in range(1, n):
        total = tokens_grad(total, i, [])

    half = total.shape[0] // 2
    top, bottom = total[:half], total[half:]
    own = jnp.where(core == 0, top, bottom)
    theirs = jnp.where(core == 0, bottom, top).astype(BF16)
    own = own + near(theirs).astype(F32)
    result = own[:rows]
    for k in range(1, far):
        block = own[k * rows : (k + 1) * rows].astype(BF16)
        result = result + from_far(block, k).astype(F32)

    grads = None
    for group in ([0], list(range(1, n))):
        if group:
            grads = weight_grads(grads, group, [theirs])
    grad_gate, grad_up, grad_down = grads
    return (result.astype(BF16), grad_gate, grad_up, grad_down)


def solution(mesh):
    placed = (P("hid", "mod"), P("hid", "mod"), P("mod", "hid"), P("mod", "hid"), P("hid", "mod"))
    return jax.shard_map(
        functools.partial(shards, mesh.shape["hid"], mesh.shape["mod"]),
        mesh=mesh,
        in_specs=placed,
        out_specs=(P("hid", "mod"), P("mod", "hid"), P("mod", "hid"), P("hid", "mod")),
        check_vma=False,
    )
```
